32 devices in a mesh: ctx: 8 (over z, x), head: 4 (over y, core).
Axes of the slice: x: 2, y: 2, z: 4, core: 2. Of those that a mesh axis runs over, the one named last changes fastest.
Arguments:
- queries: bfloat16 [4096, 4096], P('ctx', 'head'), may hold values from -200 to 200
- keys_values: bfloat16 [2, 4096, 4096], P(None, 'ctx', 'head'), may hold values from -7 to 7
- w_out: bfloat16 [4096, 4096], P('head'), may hold values from -0.09375 to 0.09375
- doc_index: int32 [4096], replicated, may hold values from 0 to 7, never falling along the last dimension, each value on 1 to 1152 neighbouring positions
Outputs:
- mixed: bfloat16 [4096, 4096], P(('ctx', 'head'))
The draws below stay inside these ranges and needn't reach their ends.
Inputs may be any that keep to these rules, and one draw needn't show every extreme that they name: `doc_index`: ids never fall along the pack; each document is a run of 1 to 1152 tokens and one has exactly 1152.
All inputs are finite; a program needn't handle non-finite values.
Results may differ from the reference program's by a relative error of at most 0.0095.
Values may be sent and summed in bfloat16 or wider, within the bound.
No kernel may reach another device: no remote copies, remote signals or barrier semaphores. Data moves between devices by JAX's collectives and lax.ppermute only.
A program may use at most 64 MiB of HBM per device.

```python
import math
import jax
import jax.numpy as jnp
import numpy as np
from jax import lax

HEADS = 32
HD = 128
D = 4096
TOK_DEV = 512
SPAN = 3
TOKENS = 4096
DOCS = 8
DOC_MOST = 1152
N_CTX = 8
N_HEAD = 4


def joint_draw(key):
    base = jax.random.fold_in(key, 7)
    first, second, third = jax.random.split(base, 3)
    width = HEADS * HD
    query_vals = jnp.clip(jax.random.normal(first, (TOKENS, width), jnp.float32), -6.0, 6.0)
    key_vals = jnp.clip(jax.random.normal(second, (TOKENS, width), jnp.float32), -6.0, 6.0)
    value_vals = jnp.clip(jax.random.normal(third, (TOKENS, width), jnp.float32), -6.0, 6.0)
    return (query_vals, jnp.stack([key_vals, value_vals]))


def draw_queries(key, part):
    return joint_draw(key)[0].astype(jnp.bfloat16)


def draw_keys_values(key, part):
    return joint_draw(key)[1].astype(jnp.bfloat16)


def block_scale(stream_key, extent, cuts, least, high):
    def one(dim, parts):
        draws = jax.random.uniform(jax.random.fold_in(jax.random.fold_in(stream_key, 6), dim), (parts,), jnp.float32, least / len(cuts), high / len(cuts))
        return jnp.repeat(jnp.exp(draws), extent[dim] // parts).reshape((-1,) + (1,) * (len(extent) - dim - 1))

    loudness = one(*cuts[0])
    for cut in cuts[1:]:
        loudness = loudness * one(*cut)
    return loudness


def split_up(number_of, total, most, slope):
    loads = [(1 << 20) // math.isqrt(grade ** slope) + 1 for grade in range(2, number_of + 1)]
    rest, given = total - most - (number_of - 1), [1] * (number_of - 1)
    while rest > 0:
        candidates = [i for i in range(number_of - 1) if given[i] < most]
        mass, remaining = sum([loads[i] for i in candidates]), rest
        for i in candidates:
            extra = min(most - given[i], max(1, remaining * loads[i] // mass), rest)
            given[i] = given[i] + extra
            rest = rest - extra
    return np.array([most] + given)


def ragged(key, number_of, total, reach, lean):
    if number_of == 2:
        one = jax.random.randint(key, (), max(1, total - reach), min(reach, total - 1) + 1)
        return jnp.stack([one, total - one])
    tallies = jnp.asarray(split_up(number_of, total, reach, lean), jnp.int32)
    pairs = (number_of - 1) // 2
    donor, taker = tallies[1:1 + 2 * pairs:2], tallies[2:2 + 2 * pairs:2]
    slack = jnp.minimum(donor - 1, reach - taker)
    shifted = jax.random.randint(jax.random.fold_in(key, 1), (pairs,), 0, 1 << 20) % (slack + 1)
    tallies = tallies.at[1:1 + 2 * pairs:2].set(donor - shifted).at[2:2 + 2 * pairs:2].set(taker + shifted)
    return tallies[jax.random.permutation(jax.random.fold_in(key, 2), number_of)]


def gaussian(stream_key, shape, scale, reach, cuts=(), kind=jnp.bfloat16):
    array = scale * jax.random.normal(stream_key, shape, jnp.float32)
    if cuts:
        array = array * block_scale(stream_key, shape, cuts, -0.22, 0.18)
    return jnp.clip(array, -reach, reach).astype(kind)


def setup_inputs(seed: int = 0) -> dict:
    arg_keys = jax.random.split(jax.random.key(seed), 5)
    return {
        "queries": draw_queries(jax.random.fold_in(arg_keys[4], 71), 0),
        "keys_values": draw_keys_values(jax.random.fold_in(arg_keys[4], 71), 0),
        "w_out": gaussian(arg_keys[2], (HEADS * HD, D), (HEADS * HD) ** -0.5, 0.09375, ((0, 4),)),
        "doc_index": jnp.searchsorted(jnp.cumsum(ragged(arg_keys[3], DOCS, TOKENS, DOC_MOST, 1)), jnp.arange(TOKENS), side="right").astype(jnp.int32),
    }


def attend_head(head, query_rows, window_kv, allowed):
    scale = HD ** -0.5
    query_head = lax.dynamic_slice_in_dim(query_rows, head * HD, HD, 1)
    key_head = lax.dynamic_slice_in_dim(window_kv[0], head * HD, HD, 1)
    value_head = lax.dynamic_slice_in_dim(window_kv[1], head * HD, HD, 1)
    raw = lax.dot_general(query_head, key_head, (((1,), (1,)), ((), ())), preferred_element_type=jnp.float32) * scale
    scores = jnp.where(allowed, raw, jnp.float32(-1e30))
    top = jnp.max(scores, axis=1, keepdims=True)
    weights = jnp.exp(scores - top)
    total = jnp.sum(weights, axis=1, keepdims=True)
    probs = weights.astype(jnp.bfloat16)
    summed = jnp.dot(probs, value_head, preferred_element_type=jnp.float32)
    return summed / total


def reference(queries, keys_values, w_out, doc_index):
    pad_rows = SPAN * TOK_DEV
    window = (SPAN + 1) * TOK_DEV
    padded_kv = jnp.concatenate([jnp.zeros((2, pad_rows, HEADS * HD), jnp.bfloat16), keys_values], axis=1)
    padded_docs = jnp.concatenate([jnp.full((pad_rows,), -1, jnp.int32), doc_index.astype(jnp.int32)])
    group_width = HEADS * HD // N_HEAD

    def one_shard(shard):
        first_row = (shard * TOK_DEV).astype(jnp.int32)
        query_rows = lax.dynamic_slice_in_dim(queries, first_row, TOK_DEV, 0)
        query_docs = lax.dynamic_slice_in_dim(doc_index.astype(jnp.int32), first_row, TOK_DEV, 0)
        query_place = first_row + jnp.arange(TOK_DEV, dtype=jnp.int32)
        window_kv = lax.dynamic_slice_in_dim(padded_kv, first_row, window, 1)
        window_docs = lax.dynamic_slice_in_dim(padded_docs, first_row, window, 0)
        key_place = first_row - pad_rows + jnp.arange(window, dtype=jnp.int32)
        allowed = (window_docs[None, :] == query_docs[:, None]) & (key_place[None, :] <= query_place[:, None])
        per_head = lax.map(lambda head: attend_head(head, query_rows, window_kv, allowed), jnp.arange(HEADS, dtype=jnp.int32))
        attended = jnp.transpose(per_head, (1, 0, 2)).reshape(TOK_DEV, HEADS * HD).astype(jnp.bfloat16)
        summed = jnp.zeros((TOK_DEV, D), jnp.float32)
        for group in range(N_HEAD):
            columns = attended[:, group * group_width:(group + 1) * group_width]
            weight_rows = w_out[group * group_width:(group + 1) * group_width]
            part = jnp.dot(columns, weight_rows, preferred_element_type=jnp.float32).astype(jnp.bfloat16)
            summed = summed + lax.optimization_barrier(part).astype(jnp.float32)
        return summed.astype(jnp.bfloat16)

    blocks = lax.map(one_shard, jnp.arange(N_CTX, dtype=jnp.int32))
    return blocks.reshape(TOKENS, D)
```

```python
import functools
import math

import jax
import jax.numpy as jnp
from jax import lax
from jax.experimental import pallas as pl
from jax.experimental.pallas import tpu as pltpu
from jax.sharding import PartitionSpec as P

HD = 128
TILE = 256
FAR_ROWS = 128
NEG = -1e30
SCALE = HD ** (-0.5) * math.log2(math.e)


def tile_bias(query_docs, key_docs, causal):
    allowed = query_docs == key_docs
    if causal:
        rows = lax.broadcasted_iota(jnp.int32, allowed.shape, 0)
        cols = lax.broadcasted_iota(jnp.int32, allowed.shape, 1)
        allowed = allowed & (cols <= rows)
    return jnp.where(allowed, jnp.float32(0), jnp.float32(NEG))


def scores_of(query, key, bias):
    raw = lax.dot_general(query, key, (((1,), (1,)), ((), ())), preferred_element_type=jnp.float32)
    return raw * SCALE + bias


def fold_tile(head, query, key, value, bias, top, total, summed):
    entry = scores_of(query, key, bias)
    old = top[head]
    new = jnp.maximum(old, jnp.max(entry, axis=1, keepdims=True))
    weights = jnp.exp2(entry - new)
    shrink = jnp.exp2(old - new)
    top[head] = new
    total[head] = total[head] * shrink + jnp.sum(weights, axis=1, keepdims=True)
    cols = pl.ds(head * HD, HD)
    summed[:, cols] = summed[:, cols] * shrink + jnp.dot(
        weights.astype(jnp.bfloat16), value, preferred_element_type=jnp.float32
    )


def local_kernel(heads, rows, pad, place, docs, q_own, q_other, kv_own, kv_other, docs_col, docs_row,
                 summed_out, stats_out, qs, kvs, top, total, summed):
    half = rows // 2
    own = pl.ds(pl.multiple_of(place[0] * half, half), half)
    other = pl.ds(pl.multiple_of((1 - place[0]) * half, half), half)
    qs[own, :] = q_own[...]
    qs[other, :] = q_other[...]
    kvs[:, own, :] = kv_own[...]
    kvs[:, other, :] = kv_other[...]

    def one_tile(step, _):
        here = pl.multiple_of(step * TILE, TILE)
        span = pl.ds(here, TILE)
        query_docs = docs_col[span, :]
        bias = tile_bias(query_docs, docs_row[:, span], True)
        for head in range(heads):
            cols = pl.ds(head * HD, HD)
            entry = scores_of(qs[span, cols], kvs[0, span, cols], bias)
            new = jnp.max(entry, axis=1, keepdims=True)
            weights = jnp.exp2(entry - new)
            top[head] = new
            total[head] = jnp.sum(weights, axis=1, keepdims=True)
            summed[:, cols] = jnp.dot(
                weights.astype(jnp.bfloat16), kvs[1, span, cols], preferred_element_type=jnp.float32
            )
        first_doc = docs[pad + here]
        live = jnp.int32(0)
        for back in range(1, rows // TILE):
            last = jnp.maximum(pad + here - (back - 1) * TILE - 1, 0)
            live += ((docs[last] == first_doc) & (step >= back)).astype(jnp.int32)

        def one_back(back, _):
            there = pl.ds(pl.multiple_of(here - (back + 1) * TILE, TILE), TILE)
            bias = tile_bias(query_docs, docs_row[:, there], False)
            for head in range(heads):
                cols = pl.ds(head * HD, HD)
                fold_tile(head, qs[span, cols], kvs[0, there, cols], kvs[1, there, cols], bias, top, total, summed)
            return 0

        lax.fori_loop(0, live, one_back, 0)
        summed_out[span, :] = summed[...]
        stats_out[span, :] = jnp.concatenate([top[h] for h in range(heads)] + [total[h] for h in range(heads)], axis=1)
        return 0

    lax.fori_loop(0, rows // TILE, one_tile, 0)


def remote_kernel(heads, rows, pad, place, docs, q_own, q_other, kv_same, kv_cross, kv_far, docs_col, docs_row,
                  summed_in, stats_in, *rest):
    outs, (qs, kvs, done, top, total, summed) = rest[:8], rest[8:]
    half = rows // 2
    side = place[0]
    own = pl.ds(pl.multiple_of(side * half, half), half)
    other = pl.ds(pl.multiple_of((1 - side) * half, half), half)
    qs[own, :] = q_own[...]
    qs[other, :] = q_other[...]
    front = pad - rows
    kvs[:, : front - FAR_ROWS, :] = jnp.zeros((2, front - FAR_ROWS, heads * HD), jnp.bfloat16)
    kvs[:, front - FAR_ROWS : front, :] = kv_far[...]
    kvs[:, pl.ds(pl.multiple_of(front + side * half, FAR_ROWS), half), :] = kv_same[...]
    kvs[:, pl.ds(pl.multiple_of(front + (1 - side) * half, FAR_ROWS), half), :] = kv_cross[...]

    def one_tile(step, _):
        here = pl.multiple_of(step * TILE, TILE)
        span = pl.ds(here, TILE)
        stats = stats_in[span, :]
        for head in range(heads):
            top[head] = stats[:, head : head + 1]
            total[head] = stats[:, heads + head : heads + head + 1]
        summed[...] = summed_in[span, :]
        first_doc = docs[pad + here]
        live = jnp.int32(0)
        for back in range(pad // TILE):
            live += (docs[pad - back * TILE - 1] == first_doc).astype(jnp.int32)

        def one_back(back, _):
            there = pl.ds(pl.multiple_of(pad - (back + 1) * TILE, TILE), TILE)
            bias = tile_bias(docs_col[span, :], docs_row[:, there], False)
            for head in range(heads):
                cols = pl.ds(head * HD, HD)
                fold_tile(head, qs[span, cols], kvs[0, there, cols], kvs[1, there, cols], bias, top, total, summed)
            return 0

        lax.fori_loop(0, live, one_back, 0)
        for head in range(heads):
            cols = pl.ds(head * HD, HD)
            done[span, cols] = (summed[:, cols] / total[head]).astype(jnp.bfloat16)
        return 0

    lax.fori_loop(0, rows // TILE, one_tile, 0)
    block = outs[0].shape[0]
    for number, out in enumerate(outs):
        out[...] = done[pl.ds(pl.multiple_of(place[1 + number] * block, block), block), :]


def project_kernel(place, same, core, cross, both, w_mine, w_other, out):
    straight = place[0] == 0
    here = jnp.concatenate([same[...], cross[...]], axis=1)
    here_turned = jnp.concatenate([cross[...], same[...]], axis=1)
    there = jnp.concatenate([core[...], both[...]], axis=1)
    there_turned = jnp.concatenate([both[...], core[...]], axis=1)
    mine = jnp.where(straight, here, here_turned)
    others = jnp.where(straight, there, there_turned)
    out[...] = (
        jnp.dot(mine, w_mine[...], preferred_element_type=jnp.float32)
        + jnp.dot(others, w_other[...], preferred_element_type=jnp.float32)
    ).astype(out.dtype)


def project(place, pieces, w_mine, w_other, kind):
    block, width = pieces[0].shape
    depth, columns = w_mine.shape
    step = 512
    whole = pl.BlockSpec((block, width), lambda i, s: (0, 0))
    slab = pl.BlockSpec((depth, step), lambda i, s: (0, i))
    return pl.pallas_call(
        project_kernel,
        grid_spec=pltpu.PrefetchScalarGridSpec(
            num_scalar_prefetch=1,
            grid=(columns // step,),
            in_specs=[whole] * 4 + [slab] * 2,
            out_specs=pl.BlockSpec((block, step), lambda i, s: (0, i)),
        ),
        out_shape=jax.ShapeDtypeStruct((block, columns), kind),
        compiler_params=pltpu.CompilerParams(vmem_limit_bytes=40 << 20),
        cost_estimate=pl.CostEstimate(
            flops=4 * block * depth * columns, bytes_accessed=4 * depth * columns, transcendentals=0
        ),
    )(place, *pieces, w_mine, w_other)


def per_device(queries, keys_values, w_out, doc_index):
    shard, width = queries.shape
    n_ctx, n_head = lax.axis_size("ctx"), lax.axis_size("head")
    me, group = lax.axis_index("ctx"), lax.axis_index("head")
    half = width // 2
    heads = half // HD
    rows = 2 * shard
    pad = rows + TILE
    side = lax.rem(me, 2)
    base = (me - side) * shard

    padded = jnp.concatenate([jnp.full((pad,), -1, jnp.int32), doc_index])
    docs = lax.dynamic_slice_in_dim(padded, base, pad + rows)
    docs_col = docs[pad:].reshape(rows, 1)
    docs_row = docs.reshape(1, pad + rows)

    swap = [(c, c ^ 1) for c in range(n_ctx)]
    hop = [(c, c + 2) for c in range(n_ctx - 2)]
    far = [(c, c + 4) for c in range(n_ctx - 4)]
    core = [(h, h ^ 1) for h in range(n_head)]
    both = [
        (c * n_head + h, (c ^ 1) * n_head + (h ^ 1)) for c in range(n_ctx) for h in range(n_head)
    ]
    far_y = [(h, h ^ 2) for h in range(n_head)]

    kv_send = lax.dynamic_slice_in_dim(keys_values, (1 - side) * half, half, 2)
    kv_own = lax.dynamic_slice_in_dim(keys_values, side * half, half, 2)
    q_send = lax.dynamic_slice_in_dim(queries, (1 - side) * half, half, 1)
    q_own = lax.dynamic_slice_in_dim(queries, side * half, half, 1)
    kv_other = lax.ppermute(kv_send, "ctx", swap)
    kv_same = lax.ppermute(kv_own, "ctx", hop)
    w_other = lax.ppermute(w_out, "head", core)
    q_other = lax.ppermute(q_send, "ctx", swap)
    kv_cross = lax.ppermute(kv_other, "ctx", hop)
    tail = jnp.where(side == 1, kv_own[:, shard - FAR_ROWS :], kv_other[:, shard - FAR_ROWS :])
    kv_far = lax.ppermute(tail, "ctx", far)

    side_1 = side.reshape(1).astype(jnp.int32)
    vmem = pl.BlockSpec(memory_space=pltpu.VMEM)
    smem = pl.BlockSpec(memory_space=pltpu.SMEM)
    state = [
        pltpu.VMEM((heads, TILE, 1), jnp.float32),
        pltpu.VMEM((heads, TILE, 1), jnp.float32),
        pltpu.VMEM((TILE, half), jnp.float32),
    ]
    summed, stats = pl.pallas_call(
        functools.partial(local_kernel, heads, rows, pad),
        in_specs=[smem, smem] + [vmem] * 6,
        out_specs=[vmem] * 2,
        out_shape=[
            jax.ShapeDtypeStruct((rows, half), jnp.float32),
            jax.ShapeDtypeStruct((rows, 2 * heads), jnp.float32),
        ],
        scratch_shapes=[
            pltpu.VMEM((rows, half), jnp.bfloat16),
            pltpu.VMEM((2, rows, half), jnp.bfloat16),
        ]
        + state,
        compiler_params=pltpu.CompilerParams(vmem_limit_bytes=40 << 20),
        cost_estimate=pl.CostEstimate(
            flops=2 * rows * rows * half, bytes_accessed=6 << 20, transcendentals=rows * rows * heads // 2
        ),
    )(side_1, docs, q_own, q_other, kv_own, kv_other, docs_col, docs_row[:, pad:])

    block = shard // n_head
    places = [side]
    for wave in range(2):
        y_part = (group // 2) ^ (1 - wave)
        for turn in range(4):
            to_side, to_core = side ^ (turn // 2), lax.rem(group, 2) ^ (turn % 2)
            places.append(to_side * n_head + y_part * 2 + to_core)
    place = jnp.stack(places).astype(jnp.int32)
    pieces = pl.pallas_call(
        functools.partial(remote_kernel, heads, rows, pad),
        in_specs=[smem, smem] + [vmem] * 9,
        out_specs=[vmem] * 8,
        out_shape=[jax.ShapeDtypeStruct((block, half), jnp.bfloat16)] * 8,
        scratch_shapes=[
            pltpu.VMEM((rows, half), jnp.bfloat16),
            pltpu.VMEM((2, pad, half), jnp.bfloat16),
            pltpu.VMEM((rows, half), jnp.bfloat16),
        ]
        + state,
        compiler_params=pltpu.CompilerParams(vmem_limit_bytes=40 << 20),
        cost_estimate=pl.CostEstimate(
            flops=2 * rows * rows * half, bytes_accessed=8 << 20, transcendentals=rows * rows * heads // 2
        ),
    )(place, docs, q_own, q_other, kv_same, kv_cross, kv_far, docs_col, docs_row[:, :pad], summed, stats)

    waves = []
    for wave in range(2):
        mine = pieces[4 * wave : 4 * wave + 4]
        waves.append(
            [
                mine[0],
                lax.ppermute(mine[1], "head", core),
                lax.ppermute(mine[2], "ctx", swap),
                lax.ppermute(mine[3], ("ctx", "head"), both),
            ]
        )
    leaving = project(side_1, waves[0], w_out, w_other, jnp.bfloat16)
    arrived = lax.ppermute(leaving, "head", far_y)
    staying = project(side_1, waves[1], w_out, w_other, jnp.float32)
    return (staying + arrived.astype(jnp.float32)).astype(jnp.bfloat16)


def solution(mesh):
    in_specs = (P("ctx", "head"), P(None, "ctx", "head"), P("head", None), P())
    out_specs = P(("ctx", "head"), None)
    return jax.shard_map(
        per_device, mesh=mesh, in_specs=in_specs, out_specs=out_specs, check_vma=False
    )
```

```python
import functools
import math

import jax
import jax.numpy as jnp
from jax import lax
from jax.experimental import pallas as pl
from jax.experimental.pallas import tpu as pltpu
from jax.sharding import PartitionSpec as P

HD = 128
TILE = 256
FAR_ROWS = 128
NEG = -1e30
SCALE = HD ** (-0.5) * math.log2(math.e)


def tile_bias(key_docs, query_docs, causal):
    allowed = key_docs == query_docs
    if causal:
        keys = lax.broadcasted_iota(jnp.int32, allowed.shape, 0)
        queries = lax.broadcasted_iota(jnp.int32, allowed.shape, 1)
        allowed = allowed & (keys <= queries)
    return jnp.where(allowed, jnp.float32(0), jnp.float32(NEG))


def scores_of(key, query, bias):
    raw = lax.dot_general(key, query, (((1,), (1,)), ((), ())), preferred_element_type=jnp.float32)
    return raw * SCALE + bias


def head_cols(head):
    return pl.ds(head * HD, HD)


def fresh_tiles(heads, keys, queries, values, bias, span, summed, stats):
    entries = [scores_of(k, q, bias) for k, q in zip(keys, queries)]
    tops = [jnp.max(e, axis=0, keepdims=True) for e in entries]
    weights = [jnp.exp2(e - t) for e, t in zip(entries, tops)]
    totals = [jnp.sum(w, axis=0, keepdims=True) for w in weights]
    sums = [
        jnp.dot(v, w.astype(jnp.bfloat16), preferred_element_type=jnp.float32)
        for v, w in zip(values, weights)
    ]
    stats[:, span] = jnp.concatenate(tops + totals, axis=0)
    for h in range(heads):
        summed[head_cols(h), span] = sums[h]


def fold_tiles(heads, keys, queries, values, bias, span, summed, stats):
    before = stats[:, span]
    olds = [summed[head_cols(h), span] for h in range(heads)]
    entries = [scores_of(k, q, bias) for k, q in zip(keys, queries)]
    tops = [
        jnp.maximum(before[h : h + 1], jnp.max(e, axis=0, keepdims=True))
        for h, e in enumerate(entries)
    ]
    shrinks = [jnp.exp2(before[h : h + 1] - t) for h, t in enumerate(tops)]
    weights = [jnp.exp2(e - t) for e, t in zip(entries, tops)]
    totals = [
        before[heads + h : heads + h + 1] * shrinks[h] + jnp.sum(w, axis=0, keepdims=True)
        for h, w in enumerate(weights)
    ]
    sums = [
        o * s + jnp.dot(v, w.astype(jnp.bfloat16), preferred_element_type=jnp.float32)
        for o, s, v, w in zip(olds, shrinks, values, weights)
    ]
    stats[:, span] = jnp.concatenate(tops + totals, axis=0)
    for h in range(heads):
        summed[head_cols(h), span] = sums[h]


def local_kernel(heads, rows, pad, place, docs, q_own, q_other, kv_own, kv_other, docs_col, docs_row,
                 summed, stats, qs, ks, vts):
    half = rows // 2
    own = pl.ds(pl.multiple_of(place[0] * half, half), half)
    other = pl.ds(pl.multiple_of((1 - place[0]) * half, half), half)
    qs[own, :] = q_own[...]
    qs[other, :] = q_other[...]
    ks[own, :] = kv_own[0]
    ks[other, :] = kv_other[0]
    for head in range(heads):
        vts[head_cols(head), own] = kv_own[1, :, head_cols(head)].T
        vts[head_cols(head), other] = kv_other[1, :, head_cols(head)].T

    def one_tile(step, _):
        here = pl.multiple_of(step * TILE, TILE)
        span = pl.ds(here, TILE)
        query_docs = docs_row[:, span]

        def operands(keys_at):
            return (
                [ks[keys_at, head_cols(h)] for h in range(heads)],
                [qs[span, head_cols(h)] for h in range(heads)],
                [vts[head_cols(h), keys_at] for h in range(heads)],
            )

        bias = tile_bias(docs_col[span, :], query_docs, True)
        fresh_tiles(heads, *operands(span), bias, span, summed, stats)
        first_doc = docs[pad + here]
        live = jnp.int32(0)
        for back in range(1, rows // TILE):
            last = jnp.maximum(pad + here - (back - 1) * TILE - 1, 0)
            live += ((docs[last] == first_doc) & (step >= back)).astype(jnp.int32)

        def one_back(back, _):
            there = pl.ds(pl.multiple_of(here - (back + 1) * TILE, TILE), TILE)
            bias = tile_bias(docs_col[there, :], query_docs, False)
            fold_tiles(heads, *operands(there), bias, span, summed, stats)
            return 0

        lax.fori_loop(0, live, one_back, 0)
        return 0

    lax.fori_loop(0, rows // TILE, one_tile, 0)


def remote_kernel(heads, rows, pad, place, docs, q_own, q_other, kv_same, kv_cross, kv_far, docs_col, docs_row,
                  summed_in, stats_in, *rest):
    outs, (qs, ks, vts, done, summed, stats) = rest[:8], rest[8:]
    half = rows // 2
    side = place[0]
    qs[pl.ds(pl.multiple_of(side * half, half), half), :] = q_own[...]
    qs[pl.ds(pl.multiple_of((1 - side) * half, half), half), :] = q_other[...]
    front = pad - rows

    def reach(query_at):
        first_doc = docs[pad + query_at]
        live = jnp.int32(0)
        for back in range(pad // TILE):
            live += (docs[pad - back * TILE - 1] == first_doc).astype(jnp.int32)
        return live

    most = reach(0)

    def place_keys(source, at, lead, size):
        ks[pl.ds(at + lead, size), :] = source[0]
        for head in range(heads):
            vts[head_cols(head), pl.ds(at + lead, size)] = source[1, :, head_cols(head)].T

    for source, offset in ((kv_same, side * half), (kv_cross, (1 - side) * half)):
        for part in range(half // TILE):
            at = pl.multiple_of(front + offset + part * TILE, TILE)

            @pl.when(most > pad // TILE - 1 - at // TILE)
            def _():
                place_keys(source.at[:, pl.ds(part * TILE, TILE)], at, 0, TILE)

    @pl.when(most > pad // TILE - 1)
    def _():
        ks[: front - FAR_ROWS, :] = jnp.zeros((front - FAR_ROWS, heads * HD), jnp.bfloat16)
        vts[:, : front - FAR_ROWS] = jnp.zeros((heads * HD, front - FAR_ROWS), jnp.bfloat16)
        place_keys(kv_far, front - FAR_ROWS, 0, FAR_ROWS)

    whole = pl.ds(0, TILE)

    def one_tile(step, _):
        here = pl.multiple_of(step * TILE, TILE)
        span = pl.ds(here, TILE)
        stats[...] = stats_in[:, span]
        summed[...] = summed_in[:, span]

        def one_back(back, _):
            there = pl.ds(pl.multiple_of(pad - (back + 1) * TILE, TILE), TILE)
            bias = tile_bias(docs_col[there, :], docs_row[:, span], False)
            fold_tiles(
                heads,
                [ks[there, head_cols(h)] for h in range(heads)],
                [qs[span, head_cols(h)] for h in range(heads)],
                [vts[head_cols(h), there] for h in range(heads)],
                bias, whole, summed, stats,
            )
            return 0

        lax.fori_loop(0, reach(here), one_back, 0)
        for head in range(heads):
            part = summed[head_cols(head), :] / stats[heads + head : heads + head + 1, :]
            done[span, head_cols(head)] = part.astype(jnp.bfloat16).T
        return 0

    lax.fori_loop(0, rows // TILE, one_tile, 0)
    block = outs[0].shape[0]
    for number, out in enumerate(outs):
        out[...] = done[pl.ds(pl.multiple_of(place[1 + number] * block, block), block), :]


def project_kernel(first, second, w_first, w_second, *rest):
    out = rest[-1]
    term = jnp.dot(first[...], w_first[...], preferred_element_type=jnp.float32) + jnp.dot(
        second[...], w_second[...], preferred_element_type=jnp.float32
    )
    if len(rest) == 2:
        term = term + rest[0][...]
    out[...] = term.astype(out.dtype)


def project_body(place, *refs):
    project_kernel(*refs)


def project(row, first, second, w_first, w_second, begun, kind):
    block, width = first.shape
    columns = w_first.shape[1]
    step = 1024
    whole = pl.BlockSpec((block, width), lambda i, s: (0, 0))
    slab = pl.BlockSpec((width, step), lambda i, s: (s[0], i))
    tile = pl.BlockSpec((block, step), lambda i, s: (0, i))
    more = [] if begun is None else [begun]
    return pl.pallas_call(
        project_body,
        grid_spec=pltpu.PrefetchScalarGridSpec(
            num_scalar_prefetch=1,
            grid=(columns // step,),
            in_specs=[whole] * 2 + [slab] * 2 + [tile] * len(more),
            out_specs=tile,
        ),
        out_shape=jax.ShapeDtypeStruct((block, columns), kind),
        compiler_params=pltpu.CompilerParams(vmem_limit_bytes=24 << 20),
        cost_estimate=pl.CostEstimate(
            flops=4 * block * width * columns, bytes_accessed=4 * width * columns, transcendentals=0
        ),
    )(row, first, second, w_first, w_second, *more)


def per_device(queries, keys_values, w_out, doc_index):
    shard, width = queries.shape
    n_ctx, n_head = lax.axis_size("ctx"), lax.axis_size("head")
    me, group = lax.axis_index("ctx"), lax.axis_index("head")
    half = width // 2
    heads = half // HD
    rows = 2 * shard
    pad = rows + TILE
    side = lax.rem(me, 2)
    base = (me - side) * shard

    padded = jnp.concatenate([jnp.full((pad,), -1, jnp.int32), doc_index])
    docs = lax.dynamic_slice_in_dim(padded, base, pad + rows)
    docs_col = docs.reshape(pad + rows, 1)
    docs_row = docs[pad:].reshape(1, rows)

    swap = [(c, c ^ 1) for c in range(n_ctx)]
    hop = [(c, c + 2) for c in range(n_ctx - 2)]
    far = [(c, c + 4) for c in range(n_ctx - 4)]
    core = [(h, h ^ 1) for h in range(n_head)]
    both = [
        (c * n_head + h, (c ^ 1) * n_head + (h ^ 1)) for c in range(n_ctx) for h in range(n_head)
    ]
    far_y = [(h, h ^ 2) for h in range(n_head)]

    kv_send = lax.dynamic_slice_in_dim(keys_values, (1 - side) * half, half, 2)
    kv_own = lax.dynamic_slice_in_dim(keys_values, side * half, half, 2)
    q_send = lax.dynamic_slice_in_dim(queries, (1 - side) * half, half, 1)
    q_own = lax.dynamic_slice_in_dim(queries, side * half, half, 1)
    kv_other = lax.ppermute(kv_send, "ctx", swap)
    kv_same = lax.ppermute(kv_own, "ctx", hop)
    w_other = lax.ppermute(w_out, "head", core)
    q_send, kv_other = lax.optimization_barrier((q_send, kv_other))
    q_other = lax.ppermute(q_send, "ctx", swap)
    kv_cross = lax.ppermute(kv_other, "ctx", hop)
    tail = jnp.where(side == 1, kv_own[:, shard - FAR_ROWS :], kv_other[:, shard - FAR_ROWS :])
    kv_far = lax.ppermute(tail, "ctx", far)

    side_1 = side.reshape(1).astype(jnp.int32)
    vmem = pl.BlockSpec(memory_space=pltpu.VMEM)
    smem = pl.BlockSpec(memory_space=pltpu.SMEM)
    summed, stats = pl.pallas_call(
        functools.partial(local_kernel, heads, rows, pad),
        in_specs=[smem, smem] + [vmem] * 6,
        out_specs=[vmem] * 2,
        out_shape=[
            jax.ShapeDtypeStruct((half, rows), jnp.float32),
            jax.ShapeDtypeStruct((2 * heads, rows), jnp.float32),
        ],
        scratch_shapes=[
            pltpu.VMEM((rows, half), jnp.bfloat16),
            pltpu.VMEM((rows, half), jnp.bfloat16),
            pltpu.VMEM((half, rows), jnp.bfloat16),
        ],
        compiler_params=pltpu.CompilerParams(vmem_limit_bytes=24 << 20),
        cost_estimate=pl.CostEstimate(
            flops=2 * rows * rows * half, bytes_accessed=6 << 20, transcendentals=rows * rows * heads // 2
        ),
    )(side_1, docs, q_own, q_other, kv_own, kv_other, docs_col[pad:], docs_row)

    block = shard // n_head
    places = [side]
    for wave in range(2):
        y_part = (group // 2) ^ (1 - wave)
        for turn in range(4):
            to_side, to_core = side ^ (turn // 2), lax.rem(group, 2) ^ (turn % 2)
            places.append(to_side * n_head + y_part * 2 + to_core)
    place = jnp.stack(places).astype(jnp.int32)
    pieces = pl.pallas_call(
        functools.partial(remote_kernel, heads, rows, pad),
        in_specs=[smem, smem] + [vmem] * 9,
        out_specs=[vmem] * 8,
        out_shape=[jax.ShapeDtypeStruct((block, half), jnp.bfloat16)] * 8,
        scratch_shapes=[
            pltpu.VMEM((rows, half), jnp.bfloat16),
            pltpu.VMEM((pad, half), jnp.bfloat16),
            pltpu.VMEM((half, pad), jnp.bfloat16),
            pltpu.VMEM((rows, half), jnp.bfloat16),
            pltpu.VMEM((half, TILE), jnp.float32),
            pltpu.VMEM((2 * heads, TILE), jnp.float32),
        ],
        compiler_params=pltpu.CompilerParams(vmem_limit_bytes=24 << 20),
        cost_estimate=pl.CostEstimate(
            flops=2 * rows * rows * half, bytes_accessed=8 << 20, transcendentals=rows * rows * heads // 2
        ),
    )(place, docs, q_own, q_other, kv_same, kv_cross, kv_far, docs_col[:pad], docs_row, summed, stats)

    here, there = side_1, 1 - side_1

    def projected(pieces, kind):
        mine = pieces[0]
        core_piece = lax.ppermute(pieces[1], "head", core)
        cross_piece = lax.ppermute(pieces[2], "ctx", swap)
        both_piece = lax.ppermute(pieces[3], ("ctx", "head"), both)
        begun = project(here, mine, core_piece, w_out, w_other, None, jnp.float32)
        return project(there, cross_piece, both_piece, w_out, w_other, begun, kind)

    leaving = projected(pieces[:4], jnp.bfloat16)
    arrived = lax.ppermute(leaving, "head", far_y)
    staying = projected(pieces[4:], jnp.float32)
    return (staying + arrived.astype(jnp.float32)).astype(jnp.bfloat16)


def solution(mesh):
    in_specs = (P("ctx", "head"), P(None, "ctx", "head"), P("head", None), P())
    out_specs = P(("ctx", "head"), None)
    return jax.shard_map(
        per_device, mesh=mesh, in_specs=in_specs, out_specs=out_specs, check_vma=False
    )
```

```python
import functools
import math

import jax
import jax.numpy as jnp
from jax import lax
from jax.experimental import pallas as pl
from jax.experimental.pallas import tpu as pltpu
from jax.sharding import PartitionSpec as P

HD = 128
COST = 1000
HOLD = 0.5
TILE = 256
FAR_ROWS = 128
NEG = -1e30
VMEM_BYTES = 16 << 20
SCALE = HD ** (-0.5) * math.log2(math.e)
F32, BF16 = jnp.float32, jnp.bfloat16
IN_HBM = pl.BlockSpec(memory_space=pltpu.HBM)
IN_VMEM = pl.BlockSpec(memory_space=pltpu.VMEM)
IN_SMEM = pl.BlockSpec(memory_space=pltpu.SMEM)
ANYWHERE = pl.BlockSpec(memory_space=pl.ANY)


def tile_bias(key_docs, query_docs, causal_from=None):
    column = jnp.broadcast_to(key_docs, (8, key_docs.shape[1])).T[:, :1]
    allowed = column == query_docs
    if causal_from is not None:
        keys = lax.broadcasted_iota(jnp.int32, allowed.shape, 0)
        queries = lax.broadcasted_iota(jnp.int32, allowed.shape, 1) + causal_from
        allowed = allowed & (keys <= queries)
    return jnp.where(allowed, jnp.float32(0), jnp.float32(NEG))


def scores_of(key, query, bias):
    raw = lax.dot_general(key, query, (((1,), (1,)), ((), ())), preferred_element_type=F32)
    return raw * SCALE + bias


def head_cols(head):
    return pl.ds(head * HD, HD)


def multiple(value, of):
    return pl.multiple_of(value, of)


def fresh_tiles(heads, jobs, summed, stats):
    entries = [scores_of(k, q, bias) for k, q, v, bias, span in jobs]
    tops = [jnp.max(e, axis=0, keepdims=True) for e in entries]
    weights = [jnp.exp2(e - t) for e, t in zip(entries, tops)]
    totals = [jnp.sum(w, axis=0, keepdims=True) for w in weights]
    sums = [
        jnp.dot(job[2], w.astype(BF16), preferred_element_type=F32) for job, w in zip(jobs, weights)
    ]
    for first in range(0, len(jobs), heads):
        span, these = jobs[first][4], slice(first, first + heads)
        stats[:, span] = jnp.concatenate(tops[these] + totals[these], axis=0)
        for h in range(heads):
            summed[head_cols(h), span] = sums[first + h]


def fold_tiles(heads, keys, queries, values, bias, span, summed, stats):
    before = stats[:, span]
    olds = [summed[head_cols(h), span] for h in range(heads)]
    entries = [scores_of(k, q, bias) for k, q in zip(keys, queries)]
    tops = [
        jnp.maximum(before[h : h + 1], jnp.max(e, axis=0, keepdims=True))
        for h, e in enumerate(entries)
    ]
    shrinks = [jnp.exp2(before[h : h + 1] - t) for h, t in enumerate(tops)]
    weights = [jnp.exp2(e - t) for e, t in zip(entries, tops)]
    totals = [
        before[heads + h : heads + h + 1] * shrinks[h] + jnp.sum(w, axis=0, keepdims=True)
        for h, w in enumerate(weights)
    ]
    sums = [
        o * s + jnp.dot(v, w.astype(BF16), preferred_element_type=F32)
        for o, s, v, w in zip(olds, shrinks, values, weights)
    ]
    stats[:, span] = jnp.concatenate(tops + totals, axis=0)
    for h in range(heads):
        summed[head_cols(h), span] = sums[h]


def transposed(heads, values, target, at):
    for head in range(heads):
        target[head_cols(head), at] = values[:, head_cols(head)].T


def started(copies):
    for copy in copies:
        copy.start()
    return copies


def waited(copies):
    for copy in copies:
        copy.wait()


def fold_keys(heads, ks, qs, vts, docs_row, query_docs, count, nearest, shift, span, summed, stats):
    def one(at, size):
        there = pl.ds(multiple(at, TILE), size)
        bias = tile_bias(docs_row[:, pl.ds(multiple(shift + at, TILE), size)], query_docs)
        fold_tiles(
            heads,
            [ks[there, head_cols(h)] for h in range(heads)],
            [qs[:, head_cols(h)] for h in range(heads)],
            [vts[head_cols(h), there] for h in range(heads)],
            bias, span, summed, stats,
        )

    def two_back(step, _):
        one(nearest - (step + 1) * 2 * TILE, 2 * TILE)
        return 0

    lax.fori_loop(0, count // 2, two_back, 0)

    @pl.when(lax.rem(count, 2) == 1)
    def _():
        one(nearest - count * TILE, TILE)


def pair_kernel(heads, shard, pad, ids, docs, docs_row, q_own, kv_own, q_other, k_other, v_other,
                summed, stats, qs, ks, vts):
    side = lax.rem(ids[0], 2)
    own = pl.ds(multiple(side * shard, shard), shard)
    other = pl.ds(multiple((1 - side) * shard, shard), shard)
    ks[own, :] = kv_own[0]
    ks[other, :] = k_other[...]
    qs[own, :] = q_own[...]
    qs[other, :] = q_other[...]
    transposed(heads, kv_own.at[1], vts, own)
    transposed(heads, v_other, vts, other)

    for step in range(shard // TILE):
        jobs = []
        for start in (0, shard):
            at = start + step * TILE
            keys, span = pl.ds(start, (step + 1) * TILE), pl.ds(at, TILE)
            bias = tile_bias(
                docs_row[:, pad + start : pad + at + TILE], docs_row[:, pad + at : pad + at + TILE],
                step * TILE,
            )
            jobs += [
                (ks[keys, head_cols(h)], qs[span, head_cols(h)], vts[head_cols(h), keys], bias, span)
                for h in range(heads)
            ]
        fresh_tiles(heads, jobs, summed, stats)

    @pl.when(docs[pad + shard - 1] == docs[pad + shard])
    def _():
        def one_tile(step, _):
            start = multiple(shard + step * TILE, TILE)
            span = pl.ds(start, TILE)
            first_doc = docs[pad + start]
            live = jnp.int32(0)
            for back in range(shard // TILE):
                live += (docs[pad + shard - back * TILE - 1] == first_doc).astype(jnp.int32)
            query_docs = docs_row[:, pl.ds(multiple(pad + start, TILE), TILE)]
            fold_keys(
                heads, ks, qs.at[span], vts, docs_row, query_docs, live, shard, pad, span, summed, stats
            )
            return 0

        lax.fori_loop(0, shard // TILE, one_tile, 0)


def remote_kernel(heads, shard, pad, wave, ids, docs, docs_row, q_own, q_other, summed_in, stats_in, *rest):
    (same, k_cross, v_cross, kv_far), rest = rest[:4], rest[4:]
    sources = ((k_cross, v_cross), (same.at[0], same.at[1]))
    outs, (qs, ks, vts, done, summed, stats, sems) = rest[:4], rest[4:]
    half = heads * HD
    side = lax.rem(ids[0], 2)
    core, y_own = lax.rem(ids[1], 2), ids[1] // 2
    y_part = 1 - y_own if wave == 0 else y_own
    part_at = multiple(y_part * TILE, TILE)
    rows = pl.ds(part_at, TILE)
    copies = [
        pltpu.make_async_copy(a, b, sems.at[i])
        for i, (a, b) in enumerate(
            (
                (q_own.at[rows, :], qs.at[side]),
                (q_other.at[rows, :], qs.at[1 - side]),
                (summed_in.at[:, rows], summed.at[0]),
                (stats_in.at[:, rows], stats.at[0]),
                (summed_in.at[:, pl.ds(multiple(shard + part_at, TILE), TILE)], summed.at[1]),
                (stats_in.at[:, pl.ds(multiple(shard + part_at, TILE), TILE)], stats.at[1]),
            )
        )
    ]
    started(copies)

    def reach(query_at):
        first_doc = docs[pad + query_at]
        live = jnp.int32(0)
        for back in range(pad // TILE):
            live += (docs[pad - back * TILE - 1] == first_doc).astype(jnp.int32)
        return live

    most = reach(part_at)

    def place_keys(keys, values, at, size):
        ks[pl.ds(at, size), :] = keys[...]
        transposed(heads, values, vts, pl.ds(at, size))

    for back in range(pad // TILE):
        at = pad - (back + 1) * TILE

        @pl.when(most > back)
        def _():
            if back == 4:
                blank = TILE - FAR_ROWS
                ks[at : at + blank, :] = jnp.zeros((blank, half), BF16)
                vts[:, at : at + blank] = jnp.zeros((half, blank), BF16)
                place_keys(kv_far.at[0], kv_far.at[1], at + blank, FAR_ROWS)
            else:
                part = pl.ds((1 - back % 2) * TILE, TILE)
                for which, (keys, values) in enumerate(sources if back < 2 else sources[::-1]):

                    @pl.when(side == which)
                    def _():
                        place_keys(keys.at[part], values.at[part], at, TILE)

    waited(copies)
    whole = pl.ds(0, TILE)

    def one_tile(step, _):
        here = multiple(step * shard + part_at, TILE)
        mine = pl.ds(multiple(step * TILE, TILE), TILE)
        query_docs = docs_row[:, pl.ds(multiple(pad + here, TILE), TILE)]

        fold_keys(
            heads, ks, qs.at[step], vts, docs_row, query_docs, reach(here), pad, 0, whole,
            summed.at[step], stats.at[step],
        )
        for head in range(heads):
            part = summed[step, head_cols(head), :] / stats[step, heads + head : heads + head + 1, :]
            done[mine, head_cols(head)] = part.astype(BF16).T
        return 0

    lax.fori_loop(0, 2, one_tile, 0)
    block = outs[0].shape[0]
    for turn, out in enumerate(outs):
        to_side = 1 - side if turn // 2 else side
        to_core = 1 - core if turn % 2 else core
        out[...] = done[pl.ds(multiple((to_side * 2 + to_core) * block, block), block), :]


def project_kernel(count, turns, ring, part, chunk, begun, ids, *refs):
    pieces, (w_near, w_other) = refs[:count], refs[count : count + 2]
    out, held, sems = refs[-3:]
    side = lax.rem(ids[0], 2)
    width = pieces[0].shape[1]
    steps = out.shape[1] // chunk
    first = part * out.shape[1]

    def copies(step):
        made = []
        for number, turn in enumerate(turns):
            source = w_other if turn % 2 else w_near
            to_side = 1 - side if turn // 2 else side
            made.append(
                pltpu.make_async_copy(
                    source.at[
                        pl.ds(multiple(to_side * width, width), width),
                        pl.ds(first + step * chunk, chunk),
                    ],
                    held.at[step % ring, number],
                    sems.at[step % ring, number],
                )
            )
        return made

    for step in range(min(ring, steps)):
        started(copies(step))
    for step in range(steps):
        waited(copies(step))
        here = slice(step * chunk, (step + 1) * chunk)
        term = refs[count + 2][:, first + step * chunk : first + (step + 1) * chunk] if begun else None
        for number in range(count):
            more = jnp.dot(pieces[number][...], held[step % ring, number], preferred_element_type=F32)
            term = more if term is None else term + more
        out[:, here] = term.astype(out.dtype)
        if step + ring < steps:
            started(copies(step + ring))


def add_kernel(staying, *refs):
    arrived, out = refs[:-1], refs[-1]
    width = arrived[0].shape[1]
    for number, part in enumerate(arrived):
        here = slice(number * width, (number + 1) * width)
        out[:, here] = (staying[:, here] + part[...].astype(F32)).astype(out.dtype)


def pass_kernel(ids, *refs):
    refs[-1][0] = ids[0]
    refs[-1][1] = ids[1]


def after(ids, arrays, micros):
    return pl.pallas_call(
        pass_kernel,
        in_specs=[IN_SMEM] + [ANYWHERE] * len(arrays),
        out_specs=IN_SMEM,
        out_shape=jax.ShapeDtypeStruct(ids.shape, ids.dtype),
        compiler_params=pltpu.CompilerParams(vmem_limit_bytes=VMEM_BYTES),
        cost_estimate=pl.CostEstimate(
            flops=int(micros * 1.1e9), bytes_accessed=1024, transcendentals=0
        ),
    )(ids, *arrays)


def call(kernel, outs, scratch, micros, specs, arrays, limit=VMEM_BYTES):
    return pl.pallas_call(
        kernel,
        in_specs=specs,
        out_specs=[IN_VMEM] * len(outs),
        out_shape=[jax.ShapeDtypeStruct(shape, kind) for shape, kind in outs],
        scratch_shapes=scratch,
        compiler_params=pltpu.CompilerParams(vmem_limit_bytes=limit),
        cost_estimate=pl.CostEstimate(
            flops=int(micros * COST), bytes_accessed=1024, transcendentals=0
        ),
    )(*arrays)


def per_device(queries, keys_values, w_out, doc_index):
    shard, width = queries.shape
    n_ctx, n_head = lax.axis_size("ctx"), lax.axis_size("head")
    me, group = lax.axis_index("ctx"), lax.axis_index("head")
    half = width // 2
    heads = half // HD
    rows = 2 * shard
    pad = rows + TILE
    block = shard // n_head

    ids = jnp.stack([me, group]).astype(jnp.int32)
    padded = jnp.concatenate([jnp.full((pad,), -1, jnp.int32), doc_index])
    docs = lax.dynamic_slice_in_dim(padded, (me // 2) * rows, pad + rows)
    docs_row = docs.reshape(1, pad + rows)

    swap = [(c, c ^ 1) for c in range(n_ctx)]
    hop = [(c, c + 2) for c in range(n_ctx - 2)]
    far = [(c, c + 4) for c in range(n_ctx - 4)]
    core = [(h, h ^ 1) for h in range(n_head)]
    both = [
        (c * n_head + h, (c ^ 1) * n_head + (h ^ 1)) for c in range(n_ctx) for h in range(n_head)
    ]
    far_y = [(h, h ^ 2) for h in range(n_head)]
    sems = pltpu.SemaphoreType.DMA
    vmem = pltpu.VMEM

    side = lax.rem(me, 2)

    def mine(array, axis):
        return lax.dynamic_slice_in_dim(array, side * half, half, axis)

    def theirs(array, axis):
        return lax.dynamic_slice_in_dim(array, (1 - side) * half, half, axis)

    kv_own = mine(keys_values, 2)
    queries, keys_values, kv_own = lax.optimization_barrier((queries, keys_values, kv_own))
    same = lax.ppermute(kv_own, "ctx", hop)
    k_other = lax.ppermute(theirs(keys_values[0], 1), "ctx", swap)
    v_other = lax.ppermute(theirs(keys_values[1], 1), "ctx", swap)
    w_other = lax.ppermute(w_out, "head", core)
    q_send, q_own = theirs(queries, 1), mine(queries, 1)
    q_send, k_other, w_other = lax.optimization_barrier((q_send, k_other, w_other))
    q_other = lax.ppermute(q_send, "ctx", swap)
    late_k = lax.ppermute(k_other, "ctx", hop)
    late_v = lax.ppermute(v_other, "ctx", hop)

    last = shard - FAR_ROWS
    tails = [kv_own[:, last:], k_other[last:], v_other[last:]]
    late_v, tails = lax.optimization_barrier((late_v, tails))

    def far_hop(own, k, v):
        return lax.ppermute(jnp.where(side == 1, own, jnp.stack([k, v])), "ctx", far)

    blocks = doc_index.reshape(-1, rows)
    kv_far = lax.cond(
        jnp.any(blocks[:-2, -1] == blocks[2:, 0]),
        far_hop,
        lambda own, k, v: jnp.zeros_like(own),
        *tails,
    )
    arrivals = [same, late_k, late_v, kv_far]
    ids_late = after(ids, [late_k], HOLD)

    summed, stats = call(
        functools.partial(pair_kernel, heads, shard, pad),
        [((half, rows), F32), ((2 * heads, rows), F32)],
        [vmem((rows, half), BF16)] * 2 + [vmem((half, rows), BF16)],
        7,
        [IN_SMEM, IN_SMEM] + [IN_VMEM] * 6,
        [ids, docs, docs_row, q_own, kv_own, q_other, k_other, v_other],
    )

    def finished(wave, stats):
        return call(
            functools.partial(remote_kernel, heads, shard, pad, wave),
            [((block, half), BF16)] * 4,
            [
                vmem((2, TILE, half), BF16),
                vmem((pad, half), BF16),
                vmem((half, pad), BF16),
                vmem((2 * TILE, half), BF16),
                vmem((2, half, TILE), F32),
                vmem((2, 2 * heads, TILE), F32),
                sems((6,)),
            ],
            5e6 if wave == 0 else 1,
            [IN_SMEM, IN_SMEM, IN_VMEM] + [IN_HBM] * 4 + [IN_VMEM] * len(arrivals),
            [ids_late, docs, docs_row, q_own, q_other, summed, stats, *arrivals],
        )

    def exchanged(pieces):
        return [
            pieces[0],
            lax.ppermute(pieces[1], "head", core),
            lax.ppermute(pieces[2], "ctx", swap),
            lax.ppermute(pieces[3], ("ctx", "head"), both),
        ]

    def project(pieces, turns, begun, kind, part, parts):
        columns = w_out.shape[1] // parts
        chunk, ring = 512, 16 // len(pieces)
        more = [] if begun is None else [begun]
        (out,) = call(
            functools.partial(
                project_kernel, len(pieces), turns, ring, part, chunk, begun is not None
            ),
            [((block, columns), kind)],
            [vmem((ring, len(pieces), half, chunk), BF16), sems((ring, len(pieces)))],
            2 * len(pieces) // parts,
            [IN_SMEM] + [IN_VMEM] * len(pieces) + [IN_HBM] * 2 + [IN_VMEM] * len(more),
            [ids, *pieces, w_out, w_other, *more],
        )
        return out

    parts = 2
    pieces = exchanged(finished(0, stats))
    begun = project(pieces[:2], (0, 1), None, F32, 0, 1)
    leaving = [project(pieces[2:], (2, 3), begun, BF16, part, parts) for part in range(parts)]
    arrived = [lax.ppermute(part, "head", far_y) for part in leaving]
    stats, leaving = lax.optimization_barrier((stats, leaving))
    pieces = exchanged(finished(1, stats))
    staying = project(pieces, (0, 1, 2, 3), None, F32, 0, 1)
    (out,) = call(
        add_kernel,
        [((block, w_out.shape[1]), BF16)],
        [],
        1,
        [IN_VMEM] * (1 + parts),
        [staying, *arrived],
    )
    return out


def solution(mesh):
    in_specs = (P("ctx", "head"), P(None, "ctx", "head"), P("head", None), P())
    out_specs = P(("ctx", "head"), None)
    return jax.shard_map(
        per_device, mesh=mesh, in_specs=in_specs, out_specs=out_specs, check_vma=False
    )
```

```python
import functools
import math

import jax
import jax.numpy as jnp
from jax import lax
from jax.experimental import pallas as pl
from jax.experimental.pallas import tpu as pltpu
from jax.sharding import PartitionSpec as P

HD = 128
COST = 1000
HOLD = 0.5
TILE = 256
FAR_ROWS = 128
NEG = -1e30
VMEM_BYTES = 16 << 20
SCALE = HD ** (-0.5) * math.log2(math.e)
F32, BF16 = jnp.float32, jnp.bfloat16
IN_HBM = pl.BlockSpec(memory_space=pltpu.HBM)
IN_VMEM = pl.BlockSpec(memory_space=pltpu.VMEM)
IN_SMEM = pl.BlockSpec(memory_space=pltpu.SMEM)
ANYWHERE = pl.BlockSpec(memory_space=pl.ANY)


def tile_bias(key_docs, query_docs, causal_from=None):
    column = jnp.broadcast_to(key_docs, (8, key_docs.shape[1])).T[:, :1]
    allowed = column == query_docs
    if causal_from is not None:
        keys = lax.broadcasted_iota(jnp.int32, allowed.shape, 0)
        queries = lax.broadcasted_iota(jnp.int32, allowed.shape, 1) + causal_from
        allowed = allowed & (keys <= queries)
    return jnp.where(allowed, jnp.float32(0), jnp.float32(NEG))


def scores_of(key, query, bias):
    raw = lax.dot_general(key, query, (((1,), (1,)), ((), ())), preferred_element_type=F32)
    return raw * SCALE + bias


def head_cols(head):
    return pl.ds(head * HD, HD)


def multiple(value, of):
    return pl.multiple_of(value, of)


def top_row(head):
    return head // 2 * 4 + head % 2


def stacked(tops, totals):
    rows = []
    for first in range(0, len(tops), 2):
        rows += tops[first : first + 2] + totals[first : first + 2]
    return jnp.concatenate(rows, axis=0)


def fresh_tiles(heads, jobs, summed, stats):
    entries = [scores_of(k, q, bias) for k, q, v, bias, span in jobs]
    tops = [jnp.max(e, axis=0, keepdims=True) for e in entries]
    weights = [jnp.exp2(e - t) for e, t in zip(entries, tops)]
    totals = [jnp.sum(w, axis=0, keepdims=True) for w in weights]
    sums = [
        jnp.dot(job[2], w.astype(BF16), preferred_element_type=F32) for job, w in zip(jobs, weights)
    ]
    for first in range(0, len(jobs), heads):
        span, these = jobs[first][4], slice(first, first + heads)
        stats[:, span] = stacked(tops[these], totals[these])
        for h in range(heads):
            summed[head_cols(h), span] = sums[first + h]


def fold_tiles(heads, keys, queries, values, bias, span, summed, stats):
    before = stats[:, span]
    olds = [summed[head_cols(h), span] for h in range(heads)]
    old_tops = [before[top_row(h) : top_row(h) + 1] for h in range(heads)]
    old_totals = [before[top_row(h) + 2 : top_row(h) + 3] for h in range(heads)]
    entries = [scores_of(k, q, bias) for k, q in zip(keys, queries)]
    tops = [
        jnp.maximum(old, jnp.max(e, axis=0, keepdims=True)) for old, e in zip(old_tops, entries)
    ]
    shrinks = [jnp.exp2(old - t) for old, t in zip(old_tops, tops)]
    weights = [jnp.exp2(e - t) for e, t in zip(entries, tops)]
    totals = [
        old * s + jnp.sum(w, axis=0, keepdims=True)
        for old, s, w in zip(old_totals, shrinks, weights)
    ]
    sums = [
        o * s + jnp.dot(v, w.astype(BF16), preferred_element_type=F32)
        for o, s, v, w in zip(olds, shrinks, values, weights)
    ]
    stats[:, span] = stacked(tops, totals)
    for h in range(heads):
        summed[head_cols(h), span] = sums[h]


def transposed(heads, values, target, at):
    for head in range(heads):
        target[head_cols(head), at] = values[:, head_cols(head)].T


def started(copies):
    for copy in copies:
        copy.start()
    return copies


def waited(copies):
    for copy in copies:
        copy.wait()


def fold_keys(heads, ks, qs, vts, docs_row, query_docs, count, nearest, shift, span, summed, stats):
    def one(at, size):
        there = pl.ds(multiple(at, TILE), size)
        bias = tile_bias(docs_row[:, pl.ds(multiple(shift + at, TILE), size)], query_docs)
        fold_tiles(
            heads,
            [ks[there, head_cols(h)] for h in range(heads)],
            [qs[:, head_cols(h)] for h in range(heads)],
            [vts[head_cols(h), there] for h in range(heads)],
            bias, span, summed, stats,
        )

    def two_back(step, _):
        one(nearest - (step + 1) * 2 * TILE, 2 * TILE)
        return 0

    lax.fori_loop(0, count // 2, two_back, 0)

    @pl.when(lax.rem(count, 2) == 1)
    def _():
        one(nearest - count * TILE, TILE)


def pair_kernel(heads, shard, pad, ids, docs, docs_row, q_own, kv_own, q_other, kv_other_a, kv_other_b,
                summed, stats, qs, ks, vts):
    side = lax.rem(ids[0], 2)
    own = pl.ds(multiple(side * shard, shard), shard)
    other = pl.ds(multiple((1 - side) * shard, shard), shard)
    ks[own, :] = kv_own[0]
    for number, part in enumerate((kv_other_a, kv_other_b)):
        cols = pl.ds(number * 2 * HD, 2 * HD)
        ks[other, cols] = part[0]
        transposed(2, part.at[1], vts.at[cols], other)
    qs[own, :] = q_own[...]
    qs[other, :] = q_other[...]
    transposed(heads, kv_own.at[1], vts, own)

    for step in range(shard // TILE):
        jobs = []
        for start in (0, shard):
            at = start + step * TILE
            keys, span = pl.ds(start, (step + 1) * TILE), pl.ds(at, TILE)
            bias = tile_bias(
                docs_row[:, pad + start : pad + at + TILE], docs_row[:, pad + at : pad + at + TILE],
                step * TILE,
            )
            jobs += [
                (ks[keys, head_cols(h)], qs[span, head_cols(h)], vts[head_cols(h), keys], bias, span)
                for h in range(heads)
            ]
        fresh_tiles(heads, jobs, summed, stats)

    @pl.when(docs[pad + shard - 1] == docs[pad + shard])
    def _():
        def one_tile(step, _):
            start = multiple(shard + step * TILE, TILE)
            span = pl.ds(start, TILE)
            first_doc = docs[pad + start]
            live = jnp.int32(0)
            for back in range(shard // TILE):
                live += (docs[pad + shard - back * TILE - 1] == first_doc).astype(jnp.int32)
            query_docs = docs_row[:, pl.ds(multiple(pad + start, TILE), TILE)]
            fold_keys(
                heads, ks, qs.at[span], vts, docs_row, query_docs, live, shard, pad, span, summed, stats
            )
            return 0

        lax.fori_loop(0, shard // TILE, one_tile, 0)


def remote_kernel(groups, shard, pad, wave, ids, docs, docs_row, q_own, q_other, summed_in, stats_in, same,
                  kv_far, *rest):
    crossed, rest = rest[: len(groups)], rest[len(groups) :]
    outs, (qs, ks, vts, done, summed, stats_all, stats, sems) = rest[:4], rest[4:]
    heads = 2 * len(groups)
    width = heads * HD
    side = lax.rem(ids[0], 2)
    core, y_own = lax.rem(ids[1], 2), ids[1] // 2
    y_part = 1 - y_own if wave == 0 else y_own
    part_at = multiple(y_part * TILE, TILE)
    rows = pl.ds(part_at, TILE)
    later = pl.ds(multiple(shard + part_at, TILE), TILE)
    cols = pl.ds(groups[0] * 2 * HD, width)
    copies = [
        pltpu.make_async_copy(a, b, sems.at[i])
        for i, (a, b) in enumerate(
            (
                (q_own.at[rows, cols], qs.at[side]),
                (q_other.at[rows, cols], qs.at[1 - side]),
                (summed_in.at[cols, rows], summed.at[0]),
                (stats_in.at[:, rows], stats_all.at[0]),
                (summed_in.at[cols, later], summed.at[1]),
                (stats_in.at[:, later], stats_all.at[1]),
            )
        )
    ]
    started(copies)

    def reach(query_at):
        first_doc = docs[pad + query_at]
        live = jnp.int32(0)
        for back in range(pad // TILE):
            live += (docs[pad - back * TILE - 1] == first_doc).astype(jnp.int32)
        return live

    most = reach(part_at)

    def place_keys(keys, values, number, at, size):
        cols = pl.ds(number * 2 * HD, 2 * HD)
        ks[pl.ds(at, size), cols] = keys[...]
        transposed(2, values, vts.at[cols], pl.ds(at, size))

    for back in range(pad // TILE):
        at = pad - (back + 1) * TILE

        @pl.when(most > back)
        def _():
            if back == 4:
                blank = TILE - FAR_ROWS
                ks[at : at + blank, :] = jnp.zeros((blank, width), BF16)
                vts[:, at : at + blank] = jnp.zeros((width, blank), BF16)
                for number, group in enumerate(groups):
                    mine = pl.ds(group * 2 * HD, 2 * HD)
                    place_keys(
                        kv_far.at[0, :, mine], kv_far.at[1, :, mine], number, at + blank, FAR_ROWS
                    )
            else:
                part = pl.ds((1 - back % 2) * TILE, TILE)

                @pl.when(side == back // 2)
                def _():
                    for number in range(len(groups)):
                        place_keys(
                            crossed[number].at[0, part], crossed[number].at[1, part], number, at, TILE
                        )

                @pl.when(side == 1 - back // 2)
                def _():
                    for number, group in enumerate(groups):
                        mine = pl.ds(group * 2 * HD, 2 * HD)
                        place_keys(same.at[0, part, mine], same.at[1, part, mine], number, at, TILE)

    waited(copies)
    for step in range(2):
        stats[step] = stats_all[step, 4 * groups[0] : 4 * groups[0] + 2 * heads, :]
    whole = pl.ds(0, TILE)

    def one_tile(step, _):
        here = multiple(step * shard + part_at, TILE)
        query_docs = docs_row[:, pl.ds(multiple(pad + here, TILE), TILE)]
        fold_keys(
            heads, ks, qs.at[step], vts, docs_row, query_docs, reach(here), pad, 0, whole,
            summed.at[step], stats.at[step],
        )
        mine = pl.ds(multiple(step * TILE, TILE), TILE)
        for head in range(heads):
            total = stats[step, top_row(head) + 2 : top_row(head) + 3, :]
            part = summed[step, head_cols(head), :] / total
            done[mine, head_cols(head)] = part.astype(BF16).T
        return 0

    lax.fori_loop(0, 2, one_tile, 0)
    block = outs[0].shape[0]
    for turn, out in enumerate(outs):
        to_side = 1 - side if turn // 2 else side
        to_core = 1 - core if turn % 2 else core
        out[...] = done[pl.ds(multiple((to_side * 2 + to_core) * block, block), block), :]


def project_kernel(places, half, ring, part, chunk, begun, ids, *refs):
    count = len(places)
    pieces, (w_near, w_other) = refs[:count], refs[count : count + 2]
    out, held, sems = refs[-3:]
    side = lax.rem(ids[0], 2)
    width = pieces[0].shape[1]
    steps = out.shape[1] // chunk
    first = part * out.shape[1]

    def copies(step):
        made = []
        for number, (turn, row) in enumerate(places):
            source = w_other if turn % 2 else w_near
            to_side = 1 - side if turn // 2 else side
            made.append(
                pltpu.make_async_copy(
                    source.at[
                        pl.ds(multiple(to_side * half + row, width), width),
                        pl.ds(first + step * chunk, chunk),
                    ],
                    held.at[step % ring, number],
                    sems.at[step % ring, number],
                )
            )
        return made

    for step in range(min(ring, steps)):
        started(copies(step))
    for step in range(steps):
        waited(copies(step))
        here = slice(step * chunk, (step + 1) * chunk)
        term = refs[count + 2][:, first + step * chunk : first + (step + 1) * chunk] if begun else None
        for number in range(count):
            more = jnp.dot(pieces[number][...], held[step % ring, number], preferred_element_type=F32)
            term = more if term is None else term + more
        out[:, here] = term.astype(out.dtype)
        if step + ring < steps:
            started(copies(step + ring))


def add_kernel(staying, *refs):
    arrived, out = refs[:-1], refs[-1]
    width = arrived[0].shape[1]
    for number, part in enumerate(arrived):
        here = slice(number * width, (number + 1) * width)
        out[:, here] = (staying[:, here] + part[...].astype(F32)).astype(out.dtype)


def pass_kernel(ids, *refs):
    refs[-1][0] = ids[0]
    refs[-1][1] = ids[1]


def after(ids, arrays, micros):
    return pl.pallas_call(
        pass_kernel,
        in_specs=[IN_SMEM] + [ANYWHERE] * len(arrays),
        out_specs=IN_SMEM,
        out_shape=jax.ShapeDtypeStruct(ids.shape, ids.dtype),
        compiler_params=pltpu.CompilerParams(vmem_limit_bytes=VMEM_BYTES),
        cost_estimate=pl.CostEstimate(
            flops=int(micros * 1.1e9), bytes_accessed=1024, transcendentals=0
        ),
    )(ids, *arrays)


def call(kernel, outs, scratch, micros, specs, arrays, limit=VMEM_BYTES):
    return pl.pallas_call(
        kernel,
        in_specs=specs,
        out_specs=[IN_VMEM] * len(outs),
        out_shape=[jax.ShapeDtypeStruct(shape, kind) for shape, kind in outs],
        scratch_shapes=scratch,
        compiler_params=pltpu.CompilerParams(vmem_limit_bytes=limit),
        cost_estimate=pl.CostEstimate(
            flops=int(micros * COST), bytes_accessed=1024, transcendentals=0
        ),
    )(*arrays)


def per_device(queries, keys_values, w_out, doc_index):
    shard, width = queries.shape
    n_ctx, n_head = lax.axis_size("ctx"), lax.axis_size("head")
    me, group = lax.axis_index("ctx"), lax.axis_index("head")
    half = width // 2
    heads = half // HD
    rows = 2 * shard
    pad = rows + TILE
    block = shard // n_head

    ids = jnp.stack([me, group]).astype(jnp.int32)
    padded = jnp.concatenate([jnp.full((pad,), -1, jnp.int32), doc_index])
    docs = lax.dynamic_slice_in_dim(padded, (me // 2) * rows, pad + rows)
    docs_row = docs.reshape(1, pad + rows)

    swap = [(c, c ^ 1) for c in range(n_ctx)]
    hop = [(c, c + 2) for c in range(n_ctx - 2)]
    far = [(c, c + 4) for c in range(n_ctx - 4)]
    core = [(h, h ^ 1) for h in range(n_head)]
    both = [
        (c * n_head + h, (c ^ 1) * n_head + (h ^ 1)) for c in range(n_ctx) for h in range(n_head)
    ]
    far_y = [(h, h ^ 2) for h in range(n_head)]
    sems = pltpu.SemaphoreType.DMA
    vmem = pltpu.VMEM

    side = lax.rem(me, 2)

    def mine(array, axis):
        return lax.dynamic_slice_in_dim(array, side * half, half, axis)

    def theirs(array, axis):
        return lax.dynamic_slice_in_dim(array, (1 - side) * half, half, axis)

    kv_own = mine(keys_values, 2)
    queries, keys_values, kv_own = lax.optimization_barrier((queries, keys_values, kv_own))
    same = lax.ppermute(kv_own, "ctx", hop)
    quarter = half // 2
    kv_other = [
        lax.ppermute(
            lax.dynamic_slice_in_dim(keys_values, (1 - side) * half + group * quarter, quarter, 2),
            "ctx",
            swap,
        )
        for group in range(2)
    ]
    w_other = lax.ppermute(w_out, "head", core)
    q_send, q_own = theirs(queries, 1), mine(queries, 1)
    q_send, kv_other[0], w_other = lax.optimization_barrier((q_send, kv_other[0], w_other))
    q_other = lax.ppermute(q_send, "ctx", swap)
    crossed = [lax.ppermute(part, "ctx", hop) for part in kv_other]

    ids_late = after(ids, crossed[:1], HOLD)

    summed, stats = call(
        functools.partial(pair_kernel, heads, shard, pad),
        [((half, rows), F32), ((2 * heads, rows), F32)],
        [vmem((rows, half), BF16)] * 2 + [vmem((half, rows), BF16)],
        7,
        [IN_SMEM, IN_SMEM] + [IN_VMEM] * 6,
        [ids, docs, docs_row, q_own, kv_own, q_other, *kv_other],
    )

    def far_hop(own, *parts):
        tail = jnp.where(side == 1, own, jnp.concatenate(parts, axis=2))
        turn = me // 4 % 2

        def pairs(first):
            groups = [[c, (c + 4) % n_ctx] for c in range(n_ctx) if c // 4 % 2 == first]
            return lax.all_to_all(
                jnp.stack([tail, tail]), "ctx", 0, 0, axis_index_groups=groups
            )[0]

        got = pairs(0)
        if n_ctx > 8:
            got = jnp.where(turn == 1, got, pairs(1))
        return got

    last = shard - FAR_ROWS
    blocks = doc_index.reshape(-1, rows)
    tails = [kv_own[:, last:]] + [part[:, last:] for part in kv_other]
    stats, tails = lax.optimization_barrier((stats, tails))
    kv_far = lax.cond(
        jnp.any(blocks[:-2, -1] == blocks[2:, 0]),
        far_hop,
        lambda own, *parts: jnp.zeros_like(own),
        *tails,
    )

    def finished(wave, groups, ids, stats):
        heads = 2 * len(groups)
        width = heads * HD
        return call(
            functools.partial(remote_kernel, groups, shard, pad, wave),
            [((block, width), BF16)] * 4,
            [
                vmem((2, TILE, width), BF16),
                vmem((pad, width), BF16),
                vmem((width, pad), BF16),
                vmem((2 * TILE, width), BF16),
                vmem((2, width, TILE), F32),
                vmem((2, 8, TILE), F32),
                vmem((2, 2 * heads, TILE), F32),
                sems((6,)),
            ],
            5e6 if wave == 0 and groups == (1,) else 1,
            [IN_SMEM, IN_SMEM, IN_VMEM] + [IN_HBM] * 4 + [IN_VMEM] * (2 + len(groups)),
            [ids, docs, docs_row, q_own, q_other, summed, stats, same, kv_far]
            + [crossed[group] for group in groups],
        )

    def exchanged(pieces):
        return [
            pieces[0],
            lax.ppermute(pieces[1], "head", core),
            lax.ppermute(pieces[2], "ctx", swap),
            lax.ppermute(pieces[3], ("ctx", "head"), both),
        ]

    def project(pieces, places, begun, kind, part, parts):
        columns = w_out.shape[1] // parts
        width = pieces[0].shape[1]
        chunk, ring = 512, min(8, 8192 // (width * len(pieces)))
        more = [] if begun is None else [begun]
        (out,) = call(
            functools.partial(project_kernel, places, half, ring, part, chunk, begun is not None),
            [((block, columns), kind)],
            [vmem((ring, len(pieces), width, chunk), BF16), sems((ring, len(pieces)))],
            1,
            [IN_SMEM] + [IN_VMEM] * len(pieces) + [IN_HBM] * 2 + [IN_VMEM] * len(more),
            [ids, *pieces, w_out, w_other, *more],
        )
        return out

    parts = 2
    early = exchanged(finished(0, (0,), ids, stats))
    late = exchanged(finished(0, (1,), ids_late, stats))
    begun = project(
        early[:2] + late[:2] + early[2:],
        ((0, 0), (1, 0), (0, quarter), (1, quarter), (2, 0), (3, 0)),
        None, F32, 0, 1,
    )
    leaving = [
        project(late[2:], ((2, quarter), (3, quarter)), begun, BF16, part, parts)
        for part in range(parts)
    ]
    arrived = [lax.ppermute(part, "head", far_y) for part in leaving]
    stats, leaving = lax.optimization_barrier((stats, leaving))
    pieces = exchanged(finished(1, (0, 1), ids_late, stats))
    staying = project(pieces, tuple((turn, 0) for turn in range(4)), None, F32, 0, 1)
    (out,) = call(
        add_kernel,
        [((block, w_out.shape[1]), BF16)],
        [],
        1,
        [IN_VMEM] * (1 + parts),
        [staying, *arrived],
    )
    return out


def solution(mesh):
    in_specs = (P("ctx", "head"), P(None, "ctx", "head"), P("head", None), P())
    out_specs = P(("ctx", "head"), None)
    return jax.shard_map(
        per_device, mesh=mesh, in_specs=in_specs, out_specs=out_specs, check_vma=False
    )
```

```python
import functools
import math

import jax
import jax.numpy as jnp
from jax import lax
from jax.experimental import pallas as pl
from jax.experimental.pallas import tpu as pltpu
from jax.sharding import PartitionSpec as P

HD = 128
COST = 1000
HOLD = 0.5
TILE = 256
FAR_ROWS = 128
NEG = -1e30
VMEM_BYTES = 16 << 20
SCALE = HD ** (-0.5) * math.log2(math.e)
F32, BF16 = jnp.float32, jnp.bfloat16
IN_HBM = pl.BlockSpec(memory_space=pltpu.HBM)
IN_VMEM = pl.BlockSpec(memory_space=pltpu.VMEM)
IN_SMEM = pl.BlockSpec(memory_space=pltpu.SMEM)
ANYWHERE = pl.BlockSpec(memory_space=pl.ANY)


def tile_bias(key_docs, query_docs, causal_from=None):
    column = jnp.broadcast_to(key_docs, (8, key_docs.shape[1])).T[:, :1]
    allowed = column == query_docs
    if causal_from is not None:
        keys = lax.broadcasted_iota(jnp.int32, allowed.shape, 0)
        queries = lax.broadcasted_iota(jnp.int32, allowed.shape, 1) + causal_from
        allowed = allowed & (keys <= queries)
    return jnp.where(allowed, jnp.float32(0), jnp.float32(NEG))


def scores_of(key, query, bias):
    raw = lax.dot_general(key, query, (((1,), (1,)), ((), ())), preferred_element_type=F32)
    return raw * SCALE + bias


def head_cols(head):
    return pl.ds(head * HD, HD)


def multiple(value, of):
    return pl.multiple_of(value, of)


def top_row(head):
    return head // 2 * 4 + head % 2


def stacked(tops, totals):
    rows = []
    for first in range(0, len(tops), 2):
        rows += tops[first : first + 2] + totals[first : first + 2]
    return jnp.concatenate(rows, axis=0)


def fresh_tiles(heads, jobs, summed, stats):
    entries = [scores_of(k, q, bias) for k, q, v, bias, span in jobs]
    tops = [jnp.max(e, axis=0, keepdims=True) for e in entries]
    weights = [jnp.exp2(e - t) for e, t in zip(entries, tops)]
    totals = [jnp.sum(w, axis=0, keepdims=True) for w in weights]
    sums = [
        jnp.dot(job[2], w.astype(BF16), preferred_element_type=F32) for job, w in zip(jobs, weights)
    ]
    for first in range(0, len(jobs), heads):
        span, these = jobs[first][4], slice(first, first + heads)
        stats[:, span] = stacked(tops[these], totals[these])
        for h in range(heads):
            summed[head_cols(h), span] = sums[first + h]


def fold_tiles(heads, keys, queries, values, bias, span, summed, stats):
    before = stats[:, span]
    olds = [summed[head_cols(h), span] for h in range(heads)]
    old_tops = [before[top_row(h) : top_row(h) + 1] for h in range(heads)]
    old_totals = [before[top_row(h) + 2 : top_row(h) + 3] for h in range(heads)]
    entries = [scores_of(k, q, bias) for k, q in zip(keys, queries)]
    tops = [
        jnp.maximum(old, jnp.max(e, axis=0, keepdims=True)) for old, e in zip(old_tops, entries)
    ]
    shrinks = [jnp.exp2(old - t) for old, t in zip(old_tops, tops)]
    weights = [jnp.exp2(e - t) for e, t in zip(entries, tops)]
    totals = [
        old * s + jnp.sum(w, axis=0, keepdims=True)
        for old, s, w in zip(old_totals, shrinks, weights)
    ]
    sums = [
        o * s + jnp.dot(v, w.astype(BF16), preferred_element_type=F32)
        for o, s, v, w in zip(olds, shrinks, values, weights)
    ]
    stats[:, span] = stacked(tops, totals)
    for h in range(heads):
        summed[head_cols(h), span] = sums[h]


def transposed(heads, values, target, at):
    for head in range(heads):
        target[head_cols(head), at] = values[:, head_cols(head)].T


def started(copies):
    for copy in copies:
        copy.start()
    return copies


def waited(copies):
    for copy in copies:
        copy.wait()


def fold_keys(heads, ks, qs, vts, docs_row, query_docs, count, nearest, shift, span, summed, stats):
    def one(at, size):
        there = pl.ds(multiple(at, TILE), size)
        bias = tile_bias(docs_row[:, pl.ds(multiple(shift + at, TILE), size)], query_docs)
        fold_tiles(
            heads,
            [ks[there, head_cols(h)] for h in range(heads)],
            [qs[:, head_cols(h)] for h in range(heads)],
            [vts[head_cols(h), there] for h in range(heads)],
            bias, span, summed, stats,
        )

    def two_back(step, _):
        one(nearest - (step + 1) * 2 * TILE, 2 * TILE)
        return 0

    lax.fori_loop(0, count // 2, two_back, 0)

    @pl.when(lax.rem(count, 2) == 1)
    def _():
        one(nearest - count * TILE, TILE)


def pair_kernel(heads, shard, pad, ids, docs, docs_row, q_own, kv_own, q_other, kv_other_a, kv_other_b,
                summed, stats, qs, ks, vts):
    side = lax.rem(ids[0], 2)
    own = pl.ds(multiple(side * shard, shard), shard)
    other = pl.ds(multiple((1 - side) * shard, shard), shard)
    ks[own, :] = kv_own[0]
    for number, part in enumerate((kv_other_a, kv_other_b)):
        cols = pl.ds(number * 2 * HD, 2 * HD)
        ks[other, cols] = part[0]
        transposed(2, part.at[1], vts.at[cols], other)
    qs[own, :] = q_own[...]
    qs[other, :] = q_other[...]
    transposed(heads, kv_own.at[1], vts, own)

    for step in range(shard // TILE):
        jobs = []
        for start in (0, shard):
            at = start + step * TILE
            keys, span = pl.ds(start, (step + 1) * TILE), pl.ds(at, TILE)
            bias = tile_bias(
                docs_row[:, pad + start : pad + at + TILE], docs_row[:, pad + at : pad + at + TILE],
                step * TILE,
            )
            jobs += [
                (ks[keys, head_cols(h)], qs[span, head_cols(h)], vts[head_cols(h), keys], bias, span)
                for h in range(heads)
            ]
        fresh_tiles(heads, jobs, summed, stats)

    @pl.when(docs[pad + shard - 1] == docs[pad + shard])
    def _():
        def one_tile(step, _):
            start = multiple(shard + step * TILE, TILE)
            span = pl.ds(start, TILE)
            first_doc = docs[pad + start]
            live = jnp.int32(0)
            for back in range(shard // TILE):
                live += (docs[pad + shard - back * TILE - 1] == first_doc).astype(jnp.int32)
            query_docs = docs_row[:, pl.ds(multiple(pad + start, TILE), TILE)]
            fold_keys(
                heads, ks, qs.at[span], vts, docs_row, query_docs, live, shard, pad, span, summed, stats
            )
            return 0

        lax.fori_loop(0, shard // TILE, one_tile, 0)


def remote_kernel(groups, shard, pad, wave, ids, docs, docs_row, q_own, q_other, summed_in, stats_in, same,
                  kv_far, *rest):
    crossed, rest = rest[: len(groups)], rest[len(groups) :]
    outs, (qs, ks, vts, done, summed, stats_all, stats, sems) = rest[:4], rest[4:]
    heads = 2 * len(groups)
    width = heads * HD
    side = lax.rem(ids[0], 2)
    core, y_own = lax.rem(ids[1], 2), ids[1] // 2
    y_part = 1 - y_own if wave == 0 else y_own
    part_at = multiple(y_part * TILE, TILE)
    rows = pl.ds(part_at, TILE)
    later = pl.ds(multiple(shard + part_at, TILE), TILE)
    cols = pl.ds(groups[0] * 2 * HD, width)
    copies = [
        pltpu.make_async_copy(a, b, sems.at[i])
        for i, (a, b) in enumerate(
            (
                (q_own.at[rows, cols], qs.at[side]),
                (q_other.at[rows, cols], qs.at[1 - side]),
                (summed_in.at[cols, rows], summed.at[0]),
                (stats_in.at[:, rows], stats_all.at[0]),
                (summed_in.at[cols, later], summed.at[1]),
                (stats_in.at[:, later], stats_all.at[1]),
            )
        )
    ]
    started(copies)

    def reach(query_at):
        first_doc = docs[pad + query_at]
        live = jnp.int32(0)
        for back in range(pad // TILE):
            live += (docs[pad - back * TILE - 1] == first_doc).astype(jnp.int32)
        return live

    most = reach(part_at)

    def place_keys(keys, values, number, at, size):
        cols = pl.ds(number * 2 * HD, 2 * HD)
        ks[pl.ds(at, size), cols] = keys[...]
        transposed(2, values, vts.at[cols], pl.ds(at, size))

    for back in range(pad // TILE):
        at = pad - (back + 1) * TILE

        @pl.when(most > back)
        def _():
            if back == 4:
                blank = TILE - FAR_ROWS
                ks[at : at + blank, :] = jnp.zeros((blank, width), BF16)
                vts[:, at : at + blank] = jnp.zeros((width, blank), BF16)
                for number, group in enumerate(groups):
                    mine = pl.ds(group * 2 * HD, 2 * HD)
                    place_keys(
                        kv_far.at[0, :, mine], kv_far.at[1, :, mine], number, at + blank, FAR_ROWS
                    )
            else:
                part = pl.ds((1 - back % 2) * TILE, TILE)

                @pl.when(side == back // 2)
                def _():
                    for number in range(len(groups)):
                        place_keys(
                            crossed[number].at[0, part], crossed[number].at[1, part], number, at, TILE
                        )

                @pl.when(side == 1 - back // 2)
                def _():
                    for number, group in enumerate(groups):
                        mine = pl.ds(group * 2 * HD, 2 * HD)
                        place_keys(same.at[0, part, mine], same.at[1, part, mine], number, at, TILE)

    waited(copies)
    for step in range(2):
        stats[step] = stats_all[step, 4 * groups[0] : 4 * groups[0] + 2 * heads, :]
    whole = pl.ds(0, TILE)

    def one_tile(step, _):
        here = multiple(step * shard + part_at, TILE)
        query_docs = docs_row[:, pl.ds(multiple(pad + here, TILE), TILE)]
        fold_keys(
            heads, ks, qs.at[step], vts, docs_row, query_docs, reach(here), pad, 0, whole,
            summed.at[step], stats.at[step],
        )
        mine = pl.ds(multiple(step * TILE, TILE), TILE)
        for head in range(heads):
            total = stats[step, top_row(head) + 2 : top_row(head) + 3, :]
            part = summed[step, head_cols(head), :] / total
            done[mine, head_cols(head)] = part.astype(BF16).T
        return 0

    lax.fori_loop(0, 2, one_tile, 0)
    block = outs[0].shape[0]
    for turn, out in enumerate(outs):
        to_side = 1 - side if turn // 2 else side
        to_core = 1 - core if turn % 2 else core
        out[...] = done[pl.ds(multiple((to_side * 2 + to_core) * block, block), block), :]


def project_kernel(places, half, ring, part, chunk, begun, ids, *refs):
    count = len(places)
    pieces, (w_near, w_other) = refs[:count], refs[count : count + 2]
    out, held, sems = refs[-3:]
    side = lax.rem(ids[0], 2)
    width = pieces[0].shape[1]
    steps = out.shape[1] // chunk
    first = part * out.shape[1]

    def copies(step):
        made = []
        for number, (turn, row) in enumerate(places):
            source = w_other if turn % 2 else w_near
            to_side = 1 - side if turn // 2 else side
            made.append(
                pltpu.make_async_copy(
                    source.at[
                        pl.ds(multiple(to_side * half + row, width), width),
                        pl.ds(first + step * chunk, chunk),
                    ],
                    held.at[step % ring, number],
                    sems.at[step % ring, number],
                )
            )
        return made

    for step in range(min(ring, steps)):
        started(copies(step))
    for step in range(steps):
        waited(copies(step))
        here = slice(step * chunk, (step + 1) * chunk)
        term = refs[count + 2][:, first + step * chunk : first + (step + 1) * chunk] if begun else None
        for number in range(count):
            more = jnp.dot(pieces[number][...], held[step % ring, number], preferred_element_type=F32)
            term = more if term is None else term + more
        out[:, here] = term.astype(out.dtype)
        if step + ring < steps:
            started(copies(step + ring))


def add_kernel(staying, *refs):
    arrived, out = refs[:-1], refs[-1]
    width = arrived[0].shape[1]
    for number, part in enumerate(arrived):
        here = slice(number * width, (number + 1) * width)
        out[:, here] = (staying[:, here] + part[...].astype(F32)).astype(out.dtype)


def pass_kernel(ids, *refs):
    refs[-1][0] = ids[0]
    refs[-1][1] = ids[1]


def after(ids, arrays, micros):
    return pl.pallas_call(
        pass_kernel,
        in_specs=[IN_SMEM] + [ANYWHERE] * len(arrays),
        out_specs=IN_SMEM,
        out_shape=jax.ShapeDtypeStruct(ids.shape, ids.dtype),
        compiler_params=pltpu.CompilerParams(vmem_limit_bytes=VMEM_BYTES),
        cost_estimate=pl.CostEstimate(
            flops=int(micros * 1.1e9), bytes_accessed=1024, transcendentals=0
        ),
    )(ids, *arrays)


def call(kernel, outs, scratch, micros, specs, arrays, limit=VMEM_BYTES):
    return pl.pallas_call(
        kernel,
        in_specs=specs,
        out_specs=[IN_VMEM] * len(outs),
        out_shape=[jax.ShapeDtypeStruct(shape, kind) for shape, kind in outs],
        scratch_shapes=scratch,
        compiler_params=pltpu.CompilerParams(vmem_limit_bytes=limit),
        cost_estimate=pl.CostEstimate(
            flops=int(micros * COST), bytes_accessed=1024, transcendentals=0
        ),
    )(*arrays)


def per_device(queries, keys_values, w_out, doc_index):
    shard, width = queries.shape
    n_ctx, n_head = lax.axis_size("ctx"), lax.axis_size("head")
    me, group = lax.axis_index("ctx"), lax.axis_index("head")
    half = width // 2
    heads = half // HD
    rows = 2 * shard
    pad = rows + TILE
    block = shard // n_head

    ids = jnp.stack([me, group]).astype(jnp.int32)
    padded = jnp.concatenate([jnp.full((pad,), -1, jnp.int32), doc_index])
    docs = lax.dynamic_slice_in_dim(padded, (me // 2) * rows, pad + rows)
    docs_row = docs.reshape(1, pad + rows)

    swap = [(c, c ^ 1) for c in range(n_ctx)]
    hop = [(c, c + 2) for c in range(n_ctx - 2)]
    far = [(c, c + 4) for c in range(n_ctx - 4)]
    core = [(h, h ^ 1) for h in range(n_head)]
    both = [
        (c * n_head + h, (c ^ 1) * n_head + (h ^ 1)) for c in range(n_ctx) for h in range(n_head)
    ]
    far_y = [(h, h ^ 2) for h in range(n_head)]
    sems = pltpu.SemaphoreType.DMA
    vmem = pltpu.VMEM

    side = lax.rem(me, 2)

    def mine(array, axis):
        return lax.dynamic_slice_in_dim(array, side * half, half, axis)

    def theirs(array, axis):
        return lax.dynamic_slice_in_dim(array, (1 - side) * half, half, axis)

    kv_own = mine(keys_values, 2)
    queries, keys_values, kv_own = lax.optimization_barrier((queries, keys_values, kv_own))
    same = lax.ppermute(kv_own, "ctx", hop)
    quarter = half // 2
    kv_other = [
        lax.ppermute(
            lax.dynamic_slice_in_dim(keys_values, (1 - side) * half + group * quarter, quarter, 2),
            "ctx",
            swap,
        )
        for group in range(2)
    ]
    w_other = lax.ppermute(w_out, "head", core)
    q_send, q_own = theirs(queries, 1), mine(queries, 1)
    q_send, kv_other[0], w_other = lax.optimization_barrier((q_send, kv_other[0], w_other))
    q_other = lax.ppermute(q_send, "ctx", swap)
    crossed = [lax.ppermute(part, "ctx", hop) for part in kv_other]

    ids_late = after(ids, crossed[:1], HOLD)

    summed, stats = call(
        functools.partial(pair_kernel, heads, shard, pad),
        [((half, rows), F32), ((2 * heads, rows), F32)],
        [vmem((rows, half), BF16)] * 2 + [vmem((half, rows), BF16)],
        7,
        [IN_SMEM, IN_SMEM] + [IN_VMEM] * 6,
        [ids, docs, docs_row, q_own, kv_own, q_other, *kv_other],
    )

    def far_hop(own, *parts):
        tail = jnp.where(side == 1, own, jnp.concatenate(parts, axis=2))
        turn = me // 4 % 2

        def pairs(first):
            groups = [[c, (c + 4) % n_ctx] for c in range(n_ctx) if c // 4 % 2 == first]
            return lax.all_to_all(
                jnp.stack([tail, tail]), "ctx", 0, 0, axis_index_groups=groups
            )[0]

        got = pairs(0)
        if n_ctx > 8:
            got = jnp.where(turn == 1, got, pairs(1))
        return got

    last = shard - FAR_ROWS
    blocks = doc_index.reshape(-1, rows)
    tails = [kv_own[:, last:]] + [part[:, last:] for part in kv_other]
    stats, tails = lax.optimization_barrier((stats, tails))
    kv_far = lax.cond(
        jnp.any(blocks[:-2, -1] == blocks[2:, 0]),
        far_hop,
        lambda own, *parts: jnp.zeros_like(own),
        *tails,
    )

    def finished(wave, groups, ids, stats):
        heads = 2 * len(groups)
        width = heads * HD
        return call(
            functools.partial(remote_kernel, groups, shard, pad, wave),
            [((block, width), BF16)] * 4,
            [
                vmem((2, TILE, width), BF16),
                vmem((pad, width), BF16),
                vmem((width, pad), BF16),
                vmem((2 * TILE, width), BF16),
                vmem((2, width, TILE), F32),
                vmem((2, 8, TILE), F32),
                vmem((2, 2 * heads, TILE), F32),
                sems((6,)),
            ],
            5e6 if wave == 0 and groups == (1,) else 1,
            [IN_SMEM, IN_SMEM, IN_VMEM] + [IN_HBM] * 4 + [IN_VMEM] * (2 + len(groups)),
            [ids, docs, docs_row, q_own, q_other, summed, stats, same, kv_far]
            + [crossed[group] for group in groups],
        )

    def exchanged(pieces):
        return [
            pieces[0],
            lax.ppermute(pieces[1], "head", core),
            lax.ppermute(pieces[2], "ctx", swap),
            lax.ppermute(pieces[3], ("ctx", "head"), both),
        ]

    def project(pieces, places, begun, kind, part, parts):
        columns = w_out.shape[1] // parts
        width = pieces[0].shape[1]
        chunk = 512 if begun is None else 1024
        ring = max(2, min(8, (4 << 20) // (width * len(pieces) * chunk)))
        more = [] if begun is None else [begun]
        (out,) = call(
            functools.partial(project_kernel, places, half, ring, part, chunk, begun is not None),
            [((block, columns), kind)],
            [vmem((ring, len(pieces), width, chunk), BF16), sems((ring, len(pieces)))],
            1,
            [IN_SMEM] + [IN_VMEM] * len(pieces) + [IN_HBM] * 2 + [IN_VMEM] * len(more),
            [ids, *pieces, w_out, w_other, *more],
        )
        return out

    parts = 2
    early = exchanged(finished(0, (0,), ids, stats))
    late = exchanged(finished(0, (1,), ids_late, stats))
    begun = project(
        early[:2] + late[:2] + early[2:],
        ((0, 0), (1, 0), (0, quarter), (1, quarter), (2, 0), (3, 0)),
        None, F32, 0, 1,
    )
    leaving = [
        project(late[2:], ((2, quarter), (3, quarter)), begun, BF16, part, parts)
        for part in range(parts)
    ]
    arrived = [lax.ppermute(part, "head", far_y) for part in leaving]
    stats, leaving = lax.optimization_barrier((stats, leaving))
    pieces = exchanged(finished(1, (0, 1), ids_late, stats))
    staying = project(pieces, tuple((turn, 0) for turn in range(4)), None, F32, 0, 1)
    (out,) = call(
        add_kernel,
        [((block, w_out.shape[1]), BF16)],
        [],
        1,
        [IN_VMEM] * (1 + parts),
        [staying, *arrived],
    )
    return out


def solution(mesh):
    in_specs = (P("ctx", "head"), P(None, "ctx", "head"), P("head", None), P())
    out_specs = P(("ctx", "head"), None)
    return jax.shard_map(
        per_device, mesh=mesh, in_specs=in_specs, out_specs=out_specs, check_vma=False
    )
```

```python
import functools
import math

import jax
import jax.numpy as jnp
from jax import lax
from jax.experimental import pallas as pl
from jax.experimental.pallas import tpu as pltpu
from jax.sharding import PartitionSpec as P

HD = 128
COST = 1000
HOLD = 0.5
TILE = 256
FAR_ROWS = 128
NEG = -1e30
VMEM_BYTES = 16 << 20
PROJECT_BYTES = 24 << 20
RING_VALUES = 13 << 19
SCALE = HD ** (-0.5) * math.log2(math.e)
F32, BF16 = jnp.float32, jnp.bfloat16
IN_HBM = pl.BlockSpec(memory_space=pltpu.HBM)
IN_VMEM = pl.BlockSpec(memory_space=pltpu.VMEM)
IN_SMEM = pl.BlockSpec(memory_space=pltpu.SMEM)
ANYWHERE = pl.BlockSpec(memory_space=pl.ANY)


def tile_bias(key_docs, query_docs, causal_from=None):
    column = jnp.broadcast_to(key_docs, (8, key_docs.shape[1])).T[:, :1]
    allowed = column == query_docs
    if causal_from is not None:
        keys = lax.broadcasted_iota(jnp.int32, allowed.shape, 0)
        queries = lax.broadcasted_iota(jnp.int32, allowed.shape, 1) + causal_from
        allowed = allowed & (keys <= queries)
    return jnp.where(allowed, jnp.float32(0), jnp.float32(NEG))


def scores_of(key, query, bias):
    raw = lax.dot_general(key, query, (((1,), (1,)), ((), ())), preferred_element_type=F32)
    return raw * SCALE + bias


def head_cols(head):
    return pl.ds(head * HD, HD)


def multiple(value, of):
    return pl.multiple_of(value, of)


def top_row(head):
    return head // 2 * 4 + head % 2


def stacked(tops, totals):
    rows = []
    for first in range(0, len(tops), 2):
        rows += tops[first : first + 2] + totals[first : first + 2]
    return jnp.concatenate(rows, axis=0)


def fresh_tiles(heads, jobs, summed, stats):
    entries = [scores_of(k, q, bias) for k, q, v, bias, span in jobs]
    tops = [jnp.max(e, axis=0, keepdims=True) for e in entries]
    weights = [jnp.exp2(e - t) for e, t in zip(entries, tops)]
    totals = [jnp.sum(w, axis=0, keepdims=True) for w in weights]
    sums = [
        jnp.dot(job[2], w.astype(BF16), preferred_element_type=F32) for job, w in zip(jobs, weights)
    ]
    for first in range(0, len(jobs), heads):
        span, these = jobs[first][4], slice(first, first + heads)
        stats[:, span] = stacked(tops[these], totals[these])
        for h in range(heads):
            summed[head_cols(h), span] = sums[first + h]


def fold_tiles(heads, keys, queries, values, bias, span, summed, stats):
    before = stats[:, span]
    olds = [summed[head_cols(h), span] for h in range(heads)]
    old_tops = [before[top_row(h) : top_row(h) + 1] for h in range(heads)]
    old_totals = [before[top_row(h) + 2 : top_row(h) + 3] for h in range(heads)]
    entries = [scores_of(k, q, bias) for k, q in zip(keys, queries)]
    tops = [
        jnp.maximum(old, jnp.max(e, axis=0, keepdims=True)) for old, e in zip(old_tops, entries)
    ]
    shrinks = [jnp.exp2(old - t) for old, t in zip(old_tops, tops)]
    weights = [jnp.exp2(e - t) for e, t in zip(entries, tops)]
    totals = [
        old * s + jnp.sum(w, axis=0, keepdims=True)
        for old, s, w in zip(old_totals, shrinks, weights)
    ]
    sums = [
        o * s + jnp.dot(v, w.astype(BF16), preferred_element_type=F32)
        for o, s, v, w in zip(olds, shrinks, values, weights)
    ]
    stats[:, span] = stacked(tops, totals)
    for h in range(heads):
        summed[head_cols(h), span] = sums[h]


def transposed(heads, values, target, at):
    for head in range(heads):
        target[head_cols(head), at] = values[:, head_cols(head)].T


def started(copies):
    for copy in copies:
        copy.start()
    return copies


def waited(copies):
    for copy in copies:
        copy.wait()


def fold_keys(heads, ks, qs, vts, docs_row, query_docs, count, nearest, shift, span, summed, stats):
    def one(at, size):
        there = pl.ds(multiple(at, TILE), size)
        bias = tile_bias(docs_row[:, pl.ds(multiple(shift + at, TILE), size)], query_docs)
        fold_tiles(
            heads,
            [ks[there, head_cols(h)] for h in range(heads)],
            [qs[:, head_cols(h)] for h in range(heads)],
            [vts[head_cols(h), there] for h in range(heads)],
            bias, span, summed, stats,
        )

    def two_back(step, _):
        one(nearest - (step + 1) * 2 * TILE, 2 * TILE)
        return 0

    lax.fori_loop(0, count // 2, two_back, 0)

    @pl.when(lax.rem(count, 2) == 1)
    def _():
        one(nearest - count * TILE, TILE)


def pair_kernel(heads, shard, pad, ids, docs, docs_row, q_own, kv_own, q_other, kv_other_a, kv_other_b,
                summed, stats, qs, ks, vts):
    side = lax.rem(ids[0], 2)
    own = pl.ds(multiple(side * shard, shard), shard)
    other = pl.ds(multiple((1 - side) * shard, shard), shard)
    ks[own, :] = kv_own[0]
    for number, part in enumerate((kv_other_a, kv_other_b)):
        cols = pl.ds(number * 2 * HD, 2 * HD)
        ks[other, cols] = part[0]
        transposed(2, part.at[1], vts.at[cols], other)
    qs[own, :] = q_own[...]
    qs[other, :] = q_other[...]
    transposed(heads, kv_own.at[1], vts, own)

    for step in range(shard // TILE):
        jobs = []
        for start in (0, shard):
            at = start + step * TILE
            keys, span = pl.ds(start, (step + 1) * TILE), pl.ds(at, TILE)
            bias = tile_bias(
                docs_row[:, pad + start : pad + at + TILE], docs_row[:, pad + at : pad + at + TILE],
                step * TILE,
            )
            jobs += [
                (ks[keys, head_cols(h)], qs[span, head_cols(h)], vts[head_cols(h), keys], bias, span)
                for h in range(heads)
            ]
        fresh_tiles(heads, jobs, summed, stats)

    @pl.when(docs[pad + shard - 1] == docs[pad + shard])
    def _():
        def one_tile(step, _):
            start = multiple(shard + step * TILE, TILE)
            span = pl.ds(start, TILE)
            first_doc = docs[pad + start]
            live = jnp.int32(0)
            for back in range(shard // TILE):
                live += (docs[pad + shard - back * TILE - 1] == first_doc).astype(jnp.int32)
            query_docs = docs_row[:, pl.ds(multiple(pad + start, TILE), TILE)]
            fold_keys(
                heads, ks, qs.at[span], vts, docs_row, query_docs, live, shard, pad, span, summed, stats
            )
            return 0

        lax.fori_loop(0, shard // TILE, one_tile, 0)


def remote_kernel(groups, shard, pad, wave, ids, docs, docs_row, q_own, q_other, summed_in, stats_in, same,
                  kv_far, *rest):
    crossed, rest = rest[: len(groups)], rest[len(groups) :]
    outs, (qs, ks, vts, done, summed, stats_all, stats, sems) = rest[:4], rest[4:]
    heads = 2 * len(groups)
    width = heads * HD
    side = lax.rem(ids[0], 2)
    core, y_own = lax.rem(ids[1], 2), ids[1] // 2
    y_part = 1 - y_own if wave == 0 else y_own
    part_at = multiple(y_part * TILE, TILE)
    rows = pl.ds(part_at, TILE)
    later = pl.ds(multiple(shard + part_at, TILE), TILE)
    cols = pl.ds(groups[0] * 2 * HD, width)
    copies = [
        pltpu.make_async_copy(a, b, sems.at[i])
        for i, (a, b) in enumerate(
            (
                (q_own.at[rows, cols], qs.at[side]),
                (q_other.at[rows, cols], qs.at[1 - side]),
                (summed_in.at[cols, rows], summed.at[0]),
                (stats_in.at[:, rows], stats_all.at[0]),
                (summed_in.at[cols, later], summed.at[1]),
                (stats_in.at[:, later], stats_all.at[1]),
            )
        )
    ]
    started(copies)

    def reach(query_at):
        first_doc = docs[pad + query_at]
        live = jnp.int32(0)
        for back in range(pad // TILE):
            live += (docs[pad - back * TILE - 1] == first_doc).astype(jnp.int32)
        return live

    most = reach(part_at)

    def place_keys(keys, values, number, at, size):
        cols = pl.ds(number * 2 * HD, 2 * HD)
        ks[pl.ds(at, size), cols] = keys[...]
        transposed(2, values, vts.at[cols], pl.ds(at, size))

    for back in range(pad // TILE):
        at = pad - (back + 1) * TILE

        @pl.when(most > back)
        def _():
            if back == 4:
                blank = TILE - FAR_ROWS
                ks[at : at + blank, :] = jnp.zeros((blank, width), BF16)
                vts[:, at : at + blank] = jnp.zeros((width, blank), BF16)
                for number, group in enumerate(groups):
                    mine = pl.ds(group * 2 * HD, 2 * HD)
                    place_keys(
                        kv_far.at[0, :, mine], kv_far.at[1, :, mine], number, at + blank, FAR_ROWS
                    )
            else:
                part = pl.ds((1 - back % 2) * TILE, TILE)

                @pl.when(side == back // 2)
                def _():
                    for number in range(len(groups)):
                        place_keys(
                            crossed[number].at[0, part], crossed[number].at[1, part], number, at, TILE
                        )

                @pl.when(side == 1 - back // 2)
                def _():
                    for number, group in enumerate(groups):
                        mine = pl.ds(group * 2 * HD, 2 * HD)
                        place_keys(same.at[0, part, mine], same.at[1, part, mine], number, at, TILE)

    waited(copies)
    for step in range(2):
        stats[step] = stats_all[step, 4 * groups[0] : 4 * groups[0] + 2 * heads, :]
    whole = pl.ds(0, TILE)

    def one_tile(step, _):
        here = multiple(step * shard + part_at, TILE)
        query_docs = docs_row[:, pl.ds(multiple(pad + here, TILE), TILE)]
        fold_keys(
            heads, ks, qs.at[step], vts, docs_row, query_docs, reach(here), pad, 0, whole,
            summed.at[step], stats.at[step],
        )
        mine = pl.ds(multiple(step * TILE, TILE), TILE)
        for head in range(heads):
            total = stats[step, top_row(head) + 2 : top_row(head) + 3, :]
            part = summed[step, head_cols(head), :] / total
            done[mine, head_cols(head)] = part.astype(BF16).T
        return 0

    lax.fori_loop(0, 2, one_tile, 0)
    block = outs[0].shape[0]
    for turn, out in enumerate(outs):
        to_side = 1 - side if turn // 2 else side
        to_core = 1 - core if turn % 2 else core
        out[...] = done[pl.ds(multiple((to_side * 2 + to_core) * block, block), block), :]


def project_kernel(places, half, ring, part, chunk, begun, ids, *refs):
    count = len(places)
    pieces, (w_near, w_other) = refs[:count], refs[count : count + 2]
    out, held, sems = refs[-3:]
    side = lax.rem(ids[0], 2)
    width = pieces[0].shape[1]
    steps = out.shape[1] // chunk
    first = part * out.shape[1]

    def copies(step):
        made = []
        for number, (turn, row) in enumerate(places):
            source = w_other if turn % 2 else w_near
            to_side = 1 - side if turn // 2 else side
            made.append(
                pltpu.make_async_copy(
                    source.at[
                        pl.ds(multiple(to_side * half + row, width), width),
                        pl.ds(first + step * chunk, chunk),
                    ],
                    held.at[step % ring, number],
                    sems.at[step % ring, number],
                )
            )
        return made

    for step in range(min(ring, steps)):
        started(copies(step))
    for step in range(steps):
        waited(copies(step))
        here = slice(step * chunk, (step + 1) * chunk)
        term = refs[count + 2][:, first + step * chunk : first + (step + 1) * chunk] if begun else None
        for number in range(count):
            more = jnp.dot(pieces[number][...], held[step % ring, number], preferred_element_type=F32)
            term = more if term is None else term + more
        out[:, here] = term.astype(out.dtype)
        if step + ring < steps:
            started(copies(step + ring))


def add_kernel(staying, *refs):
    arrived, out = refs[:-1], refs[-1]
    width = arrived[0].shape[1]
    for number, part in enumerate(arrived):
        here = slice(number * width, (number + 1) * width)
        out[:, here] = (staying[:, here] + part[...].astype(F32)).astype(out.dtype)


def pass_kernel(ids, *refs):
    refs[-1][0] = ids[0]
    refs[-1][1] = ids[1]


def after(ids, arrays, micros):
    return pl.pallas_call(
        pass_kernel,
        in_specs=[IN_SMEM] + [ANYWHERE] * len(arrays),
        out_specs=IN_SMEM,
        out_shape=jax.ShapeDtypeStruct(ids.shape, ids.dtype),
        compiler_params=pltpu.CompilerParams(vmem_limit_bytes=VMEM_BYTES),
        cost_estimate=pl.CostEstimate(
            flops=int(micros * 1.1e9), bytes_accessed=1024, transcendentals=0
        ),
    )(ids, *arrays)


def call(kernel, outs, scratch, micros, specs, arrays, limit=VMEM_BYTES):
    return pl.pallas_call(
        kernel,
        in_specs=specs,
        out_specs=[IN_VMEM] * len(outs),
        out_shape=[jax.ShapeDtypeStruct(shape, kind) for shape, kind in outs],
        scratch_shapes=scratch,
        compiler_params=pltpu.CompilerParams(vmem_limit_bytes=limit),
        cost_estimate=pl.CostEstimate(
            flops=int(micros * COST), bytes_accessed=1024, transcendentals=0
        ),
    )(*arrays)


def per_device(queries, keys_values, w_out, doc_index):
    shard, width = queries.shape
    n_ctx, n_head = lax.axis_size("ctx"), lax.axis_size("head")
    me, group = lax.axis_index("ctx"), lax.axis_index("head")
    half = width // 2
    heads = half // HD
    rows = 2 * shard
    pad = rows + TILE
    block = shard // n_head

    ids = jnp.stack([me, group]).astype(jnp.int32)
    padded = jnp.concatenate([jnp.full((pad,), -1, jnp.int32), doc_index])
    docs = lax.dynamic_slice_in_dim(padded, (me // 2) * rows, pad + rows)
    docs_row = docs.reshape(1, pad + rows)

    swap = [(c, c ^ 1) for c in range(n_ctx)]
    hop = [(c, c + 2) for c in range(n_ctx - 2)]
    far = [(c, c + 4) for c in range(n_ctx - 4)]
    core = [(h, h ^ 1) for h in range(n_head)]
    both = [
        (c * n_head + h, (c ^ 1) * n_head + (h ^ 1)) for c in range(n_ctx) for h in range(n_head)
    ]
    far_y = [(h, h ^ 2) for h in range(n_head)]
    sems = pltpu.SemaphoreType.DMA
    vmem = pltpu.VMEM

    side = lax.rem(me, 2)

    def mine(array, axis):
        return lax.dynamic_slice_in_dim(array, side * half, half, axis)

    def theirs(array, axis):
        return lax.dynamic_slice_in_dim(array, (1 - side) * half, half, axis)

    kv_own = mine(keys_values, 2)
    queries, keys_values, kv_own = lax.optimization_barrier((queries, keys_values, kv_own))
    same = lax.ppermute(kv_own, "ctx", hop)
    quarter = half // 2
    kv_other = [
        lax.ppermute(
            lax.dynamic_slice_in_dim(keys_values, (1 - side) * half + group * quarter, quarter, 2),
            "ctx",
            swap,
        )
        for group in range(2)
    ]
    w_other = lax.ppermute(w_out, "head", core)
    q_send, q_own = theirs(queries, 1), mine(queries, 1)
    q_send, kv_other[0], w_other = lax.optimization_barrier((q_send, kv_other[0], w_other))
    q_other = lax.ppermute(q_send, "ctx", swap)
    crossed = [lax.ppermute(part, "ctx", hop) for part in kv_other]

    ids_late = after(ids, crossed[:1], HOLD)

    summed, stats = call(
        functools.partial(pair_kernel, heads, shard, pad),
        [((half, rows), F32), ((2 * heads, rows), F32)],
        [vmem((rows, half), BF16)] * 2 + [vmem((half, rows), BF16)],
        7,
        [IN_SMEM, IN_SMEM] + [IN_VMEM] * 6,
        [ids, docs, docs_row, q_own, kv_own, q_other, *kv_other],
    )

    def far_hop(own, *parts):
        tail = jnp.where(side == 1, own, jnp.concatenate(parts, axis=2))
        turn = me // 4 % 2

        def pairs(first):
            groups = [[c, (c + 4) % n_ctx] for c in range(n_ctx) if c // 4 % 2 == first]
            return lax.all_to_all(
                jnp.stack([tail, tail]), "ctx", 0, 0, axis_index_groups=groups
            )[0]

        got = pairs(0)
        if n_ctx > 8:
            got = jnp.where(turn == 1, got, pairs(1))
        return got

    last = shard - FAR_ROWS
    blocks = doc_index.reshape(-1, rows)
    tails = [kv_own[:, last:]] + [part[:, last:] for part in kv_other]
    stats, tails = lax.optimization_barrier((stats, tails))
    kv_far = lax.cond(
        jnp.any(blocks[:-2, -1] == blocks[2:, 0]),
        far_hop,
        lambda own, *parts: jnp.zeros_like(own),
        *tails,
    )

    def finished(wave, groups, ids, stats):
        heads = 2 * len(groups)
        width = heads * HD
        return call(
            functools.partial(remote_kernel, groups, shard, pad, wave),
            [((block, width), BF16)] * 4,
            [
                vmem((2, TILE, width), BF16),
                vmem((pad, width), BF16),
                vmem((width, pad), BF16),
                vmem((2 * TILE, width), BF16),
                vmem((2, width, TILE), F32),
                vmem((2, 8, TILE), F32),
                vmem((2, 2 * heads, TILE), F32),
                sems((6,)),
            ],
            5e6 if wave == 0 and groups == (1,) else 1,
            [IN_SMEM, IN_SMEM, IN_VMEM] + [IN_HBM] * 4 + [IN_VMEM] * (2 + len(groups)),
            [ids, docs, docs_row, q_own, q_other, summed, stats, same, kv_far]
            + [crossed[group] for group in groups],
        )

    def exchanged(pieces):
        return [
            pieces[0],
            lax.ppermute(pieces[1], "head", core),
            lax.ppermute(pieces[2], "ctx", swap),
            lax.ppermute(pieces[3], ("ctx", "head"), both),
        ]

    def project(pieces, places, begun, kind, part, parts):
        columns = w_out.shape[1] // parts
        width = pieces[0].shape[1]
        chunk = 512 if begun is None else 1024
        ring = max(2, min(8, RING_VALUES // (width * len(pieces) * chunk)))
        more = [] if begun is None else [begun]
        (out,) = call(
            functools.partial(project_kernel, places, half, ring, part, chunk, begun is not None),
            [((block, columns), kind)],
            [vmem((ring, len(pieces), width, chunk), BF16), sems((ring, len(pieces)))],
            1,
            [IN_SMEM] + [IN_VMEM] * len(pieces) + [IN_HBM] * 2 + [IN_VMEM] * len(more),
            [ids, *pieces, w_out, w_other, *more],
            PROJECT_BYTES,
        )
        return out

    parts = 2
    early = exchanged(finished(0, (0,), ids, stats))
    late = exchanged(finished(0, (1,), ids_late, stats))
    begun = project(
        early[:2] + late[:2] + early[2:],
        ((0, 0), (1, 0), (0, quarter), (1, quarter), (2, 0), (3, 0)),
        None, F32, 0, 1,
    )
    leaving = [
        project(late[2:], ((2, quarter), (3, quarter)), begun, BF16, part, parts)
        for part in range(parts)
    ]
    arrived = [lax.ppermute(part, "head", far_y) for part in leaving]
    stats, leaving = lax.optimization_barrier((stats, leaving))
    pieces = exchanged(finished(1, (0, 1), ids_late, stats))
    staying = project(pieces, tuple((turn, 0) for turn in range(4)), None, F32, 0, 1)
    (out,) = call(
        add_kernel,
        [((block, w_out.shape[1]), BF16)],
        [],
        1,
        [IN_VMEM] * (1 + parts),
        [staying, *arrived],
    )
    return out


def solution(mesh):
    in_specs = (P("ctx", "head"), P(None, "ctx", "head"), P("head", None), P())
    out_specs = P(("ctx", "head"), None)
    return jax.shard_map(
        per_device, mesh=mesh, in_specs=in_specs, out_specs=out_specs, check_vma=False
    )
```

```python
import functools
import math

import jax
import jax.numpy as jnp
from jax import lax
from jax.experimental import pallas as pl
from jax.experimental.pallas import tpu as pltpu
from jax.sharding import PartitionSpec as P

HD = 128
COST = 1000
HOLD = 0.5
TILE = 256
FAR_ROWS = 128
NEG = -1e30
VMEM_BYTES = 16 << 20
PROJECT_BYTES = 24 << 20
RING_VALUES = 13 << 19
SCALE = HD ** (-0.5) * math.log2(math.e)
F32, BF16 = jnp.float32, jnp.bfloat16
IN_HBM = pl.BlockSpec(memory_space=pltpu.HBM)
IN_VMEM = pl.BlockSpec(memory_space=pltpu.VMEM)
IN_SMEM = pl.BlockSpec(memory_space=pltpu.SMEM)
ANYWHERE = pl.BlockSpec(memory_space=pl.ANY)


def tile_bias(key_docs, query_docs, causal_from=None):
    column = jnp.broadcast_to(key_docs, (8, key_docs.shape[1])).T[:, :1]
    allowed = column == query_docs
    if causal_from is not None:
        keys = lax.broadcasted_iota(jnp.int32, allowed.shape, 0)
        queries = lax.broadcasted_iota(jnp.int32, allowed.shape, 1) + causal_from
        allowed = allowed & (keys <= queries)
    return jnp.where(allowed, jnp.float32(0), jnp.float32(NEG))


def scores_of(key, query, bias):
    raw = lax.dot_general(key, query, (((1,), (1,)), ((), ())), preferred_element_type=F32)
    return raw * SCALE + bias


def head_cols(head):
    return pl.ds(head * HD, HD)


def multiple(value, of):
    return pl.multiple_of(value, of)


def top_row(head):
    return head // 2 * 4 + head % 2


def stacked(tops, totals):
    rows = []
    for first in range(0, len(tops), 2):
        rows += tops[first : first + 2] + totals[first : first + 2]
    return jnp.concatenate(rows, axis=0)


def fresh_tiles(heads, jobs, summed, stats):
    entries = [scores_of(k, q, bias) for k, q, v, bias, span in jobs]
    tops = [jnp.max(e, axis=0, keepdims=True) for e in entries]
    weights = [jnp.exp2(e - t) for e, t in zip(entries, tops)]
    totals = [jnp.sum(w, axis=0, keepdims=True) for w in weights]
    sums = [
        jnp.dot(job[2], w.astype(BF16), preferred_element_type=F32) for job, w in zip(jobs, weights)
    ]
    for first in range(0, len(jobs), heads):
        span, these = jobs[first][4], slice(first, first + heads)
        stats[:, span] = stacked(tops[these], totals[these])
        for h in range(heads):
            summed[head_cols(h), span] = sums[first + h]


def fold_tiles(heads, keys, queries, values, bias, span, summed, stats):
    before = stats[:, span]
    olds = [summed[head_cols(h), span] for h in range(heads)]
    old_tops = [before[top_row(h) : top_row(h) + 1] for h in range(heads)]
    old_totals = [before[top_row(h) + 2 : top_row(h) + 3] for h in range(heads)]
    entries = [scores_of(k, q, bias) for k, q in zip(keys, queries)]
    tops = [
        jnp.maximum(old, jnp.max(e, axis=0, keepdims=True)) for old, e in zip(old_tops, entries)
    ]
    shrinks = [jnp.exp2(old - t) for old, t in zip(old_tops, tops)]
    weights = [jnp.exp2(e - t) for e, t in zip(entries, tops)]
    totals = [
        old * s + jnp.sum(w, axis=0, keepdims=True)
        for old, s, w in zip(old_totals, shrinks, weights)
    ]
    sums = [
        o * s + jnp.dot(v, w.astype(BF16), preferred_element_type=F32)
        for o, s, v, w in zip(olds, shrinks, values, weights)
    ]
    stats[:, span] = stacked(tops, totals)
    for h in range(heads):
        summed[head_cols(h), span] = sums[h]


def transposed(heads, values, target, at):
    for head in range(heads):
        target[head_cols(head), at] = values[:, head_cols(head)].T


def started(copies):
    for copy in copies:
        copy.start()
    return copies


def waited(copies):
    for copy in copies:
        copy.wait()


def fold_keys(heads, ks, qs, vts, docs_row, query_docs, count, nearest, shift, span, summed, stats):
    def one(at, size):
        there = pl.ds(multiple(at, TILE), size)
        bias = tile_bias(docs_row[:, pl.ds(multiple(shift + at, TILE), size)], query_docs)
        fold_tiles(
            heads,
            [ks[there, head_cols(h)] for h in range(heads)],
            [qs[:, head_cols(h)] for h in range(heads)],
            [vts[head_cols(h), there] for h in range(heads)],
            bias, span, summed, stats,
        )

    def two_back(step, _):
        one(nearest - (step + 1) * 2 * TILE, 2 * TILE)
        return 0

    lax.fori_loop(0, count // 2, two_back, 0)

    @pl.when(lax.rem(count, 2) == 1)
    def _():
        one(nearest - count * TILE, TILE)


def pair_kernel(heads, shard, pad, ids, docs, docs_row, q_own, kv_own, q_other, kv_other_a, kv_other_b,
                summed, stats, qs, ks, vts):
    side = lax.rem(ids[0], 2)
    own = pl.ds(multiple(side * shard, shard), shard)
    other = pl.ds(multiple((1 - side) * shard, shard), shard)
    ks[own, :] = kv_own[0]
    for number, part in enumerate((kv_other_a, kv_other_b)):
        cols = pl.ds(number * 2 * HD, 2 * HD)
        ks[other, cols] = part[0]
        transposed(2, part.at[1], vts.at[cols], other)
    qs[own, :] = q_own[...]
    qs[other, :] = q_other[...]
    transposed(heads, kv_own.at[1], vts, own)

    for step in range(shard // TILE):
        jobs = []
        for start in (0, shard):
            at = start + step * TILE
            keys, span = pl.ds(start, (step + 1) * TILE), pl.ds(at, TILE)
            bias = tile_bias(
                docs_row[:, pad + start : pad + at + TILE], docs_row[:, pad + at : pad + at + TILE],
                step * TILE,
            )
            jobs += [
                (ks[keys, head_cols(h)], qs[span, head_cols(h)], vts[head_cols(h), keys], bias, span)
                for h in range(heads)
            ]
        fresh_tiles(heads, jobs, summed, stats)

    @pl.when(docs[pad + shard - 1] == docs[pad + shard])
    def _():
        def one_tile(step, _):
            start = multiple(shard + step * TILE, TILE)
            span = pl.ds(start, TILE)
            first_doc = docs[pad + start]
            live = jnp.int32(0)
            for back in range(shard // TILE):
                live += (docs[pad + shard - back * TILE - 1] == first_doc).astype(jnp.int32)
            query_docs = docs_row[:, pl.ds(multiple(pad + start, TILE), TILE)]
            fold_keys(
                heads, ks, qs.at[span], vts, docs_row, query_docs, live, shard, pad, span, summed, stats
            )
            return 0

        lax.fori_loop(0, shard // TILE, one_tile, 0)


def remote_kernel(groups, shard, pad, wave, ids, docs, docs_row, q_own, q_other, summed_in, stats_in, same,
                  kv_far, *rest):
    crossed, rest = rest[: len(groups)], rest[len(groups) :]
    outs, (qs, ks, vts, done, summed, stats_all, stats, sems) = rest[:4], rest[4:]
    heads = 2 * len(groups)
    width = heads * HD
    side = lax.rem(ids[0], 2)
    core, y_own = lax.rem(ids[1], 2), ids[1] // 2
    y_part = 1 - y_own if wave == 0 else y_own
    part_at = multiple(y_part * TILE, TILE)
    rows = pl.ds(part_at, TILE)
    later = pl.ds(multiple(shard + part_at, TILE), TILE)
    cols = pl.ds(groups[0] * 2 * HD, width)
    copies = [
        pltpu.make_async_copy(a, b, sems.at[i])
        for i, (a, b) in enumerate(
            (
                (q_own.at[rows, cols], qs.at[side]),
                (q_other.at[rows, cols], qs.at[1 - side]),
                (summed_in.at[cols, rows], summed.at[0]),
                (stats_in.at[:, rows], stats_all.at[0]),
                (summed_in.at[cols, later], summed.at[1]),
                (stats_in.at[:, later], stats_all.at[1]),
            )
        )
    ]
    started(copies)

    def reach(query_at):
        first_doc = docs[pad + query_at]
        live = jnp.int32(0)
        for back in range(pad // TILE):
            live += (docs[pad - back * TILE - 1] == first_doc).astype(jnp.int32)
        return live

    most = reach(part_at)

    def place_keys(keys, values, number, at, size):
        cols = pl.ds(number * 2 * HD, 2 * HD)
        ks[pl.ds(at, size), cols] = keys[...]
        transposed(2, values, vts.at[cols], pl.ds(at, size))

    for back in range(pad // TILE):
        at = pad - (back + 1) * TILE

        @pl.when(most > back)
        def _():
            if back == 4:
                blank = TILE - FAR_ROWS
                ks[at : at + blank, :] = jnp.zeros((blank, width), BF16)
                vts[:, at : at + blank] = jnp.zeros((width, blank), BF16)
                for number, group in enumerate(groups):
                    mine = pl.ds(group * 2 * HD, 2 * HD)
                    place_keys(
                        kv_far.at[0, :, mine], kv_far.at[1, :, mine], number, at + blank, FAR_ROWS
                    )
            else:
                part = pl.ds((1 - back % 2) * TILE, TILE)

                @pl.when(side == back // 2)
                def _():
                    for number in range(len(groups)):
                        place_keys(
                            crossed[number].at[0, part], crossed[number].at[1, part], number, at, TILE
                        )

                @pl.when(side == 1 - back // 2)
                def _():
                    for number, group in enumerate(groups):
                        mine = pl.ds(group * 2 * HD, 2 * HD)
                        place_keys(same.at[0, part, mine], same.at[1, part, mine], number, at, TILE)

    waited(copies)
    for step in range(2):
        stats[step] = stats_all[step, 4 * groups[0] : 4 * groups[0] + 2 * heads, :]
    whole = pl.ds(0, TILE)

    def one_tile(step, _):
        here = multiple(step * shard + part_at, TILE)
        query_docs = docs_row[:, pl.ds(multiple(pad + here, TILE), TILE)]
        fold_keys(
            heads, ks, qs.at[step], vts, docs_row, query_docs, reach(here), pad, 0, whole,
            summed.at[step], stats.at[step],
        )
        mine = pl.ds(multiple(step * TILE, TILE), TILE)
        for head in range(heads):
            total = stats[step, top_row(head) + 2 : top_row(head) + 3, :]
            part = summed[step, head_cols(head), :] * (1.0 / total)
            done[mine, head_cols(head)] = part.astype(BF16).T
        return 0

    lax.fori_loop(0, 2, one_tile, 0)
    block = outs[0].shape[0]
    for turn, out in enumerate(outs):
        to_side = 1 - side if turn // 2 else side
        to_core = 1 - core if turn % 2 else core
        out[...] = done[pl.ds(multiple((to_side * 2 + to_core) * block, block), block), :]


def project_kernel(places, half, ring, part, chunk, begun, ids, *refs):
    count = len(places)
    pieces, (w_near, w_other) = refs[:count], refs[count : count + 2]
    out, held, sems = refs[-3:]
    side = lax.rem(ids[0], 2)
    width = pieces[0].shape[1]
    steps = out.shape[1] // chunk
    first = part * out.shape[1]

    def copies(step):
        made = []
        for number, (turn, row) in enumerate(places):
            source = w_other if turn % 2 else w_near
            to_side = 1 - side if turn // 2 else side
            made.append(
                pltpu.make_async_copy(
                    source.at[
                        pl.ds(multiple(to_side * half + row, width), width),
                        pl.ds(first + step * chunk, chunk),
                    ],
                    held.at[step % ring, number],
                    sems.at[step % ring, number],
                )
            )
        return made

    for step in range(min(ring, steps)):
        started(copies(step))
    for step in range(steps):
        waited(copies(step))
        here = slice(step * chunk, (step + 1) * chunk)
        term = refs[count + 2][:, first + step * chunk : first + (step + 1) * chunk] if begun else None
        for number in range(count):
            more = jnp.dot(pieces[number][...], held[step % ring, number], preferred_element_type=F32)
            term = more if term is None else term + more
        out[:, here] = term.astype(out.dtype)
        if step + ring < steps:
            started(copies(step + ring))


def add_kernel(staying, *refs):
    arrived, out = refs[:-1], refs[-1]
    width = arrived[0].shape[1]
    for number, part in enumerate(arrived):
        here = slice(number * width, (number + 1) * width)
        out[:, here] = (staying[:, here] + part[...].astype(F32)).astype(out.dtype)


def pass_kernel(ids, *refs):
    refs[-1][0] = ids[0]
    refs[-1][1] = ids[1]


def after(ids, arrays, micros):
    return pl.pallas_call(
        pass_kernel,
        in_specs=[IN_SMEM] + [ANYWHERE] * len(arrays),
        out_specs=IN_SMEM,
        out_shape=jax.ShapeDtypeStruct(ids.shape, ids.dtype),
        compiler_params=pltpu.CompilerParams(vmem_limit_bytes=VMEM_BYTES),
        cost_estimate=pl.CostEstimate(
            flops=int(micros * 1.1e9), bytes_accessed=1024, transcendentals=0
        ),
    )(ids, *arrays)


def call(kernel, outs, scratch, micros, specs, arrays, limit=VMEM_BYTES):
    return pl.pallas_call(
        kernel,
        in_specs=specs,
        out_specs=[IN_VMEM] * len(outs),
        out_shape=[jax.ShapeDtypeStruct(shape, kind) for shape, kind in outs],
        scratch_shapes=scratch,
        compiler_params=pltpu.CompilerParams(vmem_limit_bytes=limit),
        cost_estimate=pl.CostEstimate(
            flops=int(micros * COST), bytes_accessed=1024, transcendentals=0
        ),
    )(*arrays)


def per_device(queries, keys_values, w_out, doc_index):
    shard, width = queries.shape
    n_ctx, n_head = lax.axis_size("ctx"), lax.axis_size("head")
    me, group = lax.axis_index("ctx"), lax.axis_index("head")
    half = width // 2
    heads = half // HD
    rows = 2 * shard
    pad = rows + TILE
    block = shard // n_head

    ids = jnp.stack([me, group]).astype(jnp.int32)
    padded = jnp.concatenate([jnp.full((pad,), -1, jnp.int32), doc_index])
    docs = lax.dynamic_slice_in_dim(padded, (me // 2) * rows, pad + rows)
    docs_row = docs.reshape(1, pad + rows)

    swap = [(c, c ^ 1) for c in range(n_ctx)]
    hop = [(c, c + 2) for c in range(n_ctx - 2)]
    far = [(c, c + 4) for c in range(n_ctx - 4)]
    core = [(h, h ^ 1) for h in range(n_head)]
    both = [
        (c * n_head + h, (c ^ 1) * n_head + (h ^ 1)) for c in range(n_ctx) for h in range(n_head)
    ]
    far_y = [(h, h ^ 2) for h in range(n_head)]
    sems = pltpu.SemaphoreType.DMA
    vmem = pltpu.VMEM

    side = lax.rem(me, 2)

    def mine(array, axis):
        return lax.dynamic_slice_in_dim(array, side * half, half, axis)

    def theirs(array, axis):
        return lax.dynamic_slice_in_dim(array, (1 - side) * half, half, axis)

    kv_own = mine(keys_values, 2)
    queries, keys_values, kv_own = lax.optimization_barrier((queries, keys_values, kv_own))
    same = lax.ppermute(kv_own, "ctx", hop)
    quarter = half // 2
    kv_other = [
        lax.ppermute(
            lax.dynamic_slice_in_dim(keys_values, (1 - side) * half + group * quarter, quarter, 2),
            "ctx",
            swap,
        )
        for group in range(2)
    ]
    w_other = lax.ppermute(w_out, "head", core)
    q_send, q_own = theirs(queries, 1), mine(queries, 1)
    q_send, kv_other[0], w_other = lax.optimization_barrier((q_send, kv_other[0], w_other))
    q_other = lax.ppermute(q_send, "ctx", swap)
    crossed = [lax.ppermute(part, "ctx", hop) for part in kv_other]

    ids_late = after(ids, crossed[:1], HOLD)

    summed, stats = call(
        functools.partial(pair_kernel, heads, shard, pad),
        [((half, rows), F32), ((2 * heads, rows), F32)],
        [vmem((rows, half), BF16)] * 2 + [vmem((half, rows), BF16)],
        7,
        [IN_SMEM, IN_SMEM] + [IN_VMEM] * 6,
        [ids, docs, docs_row, q_own, kv_own, q_other, *kv_other],
    )

    def far_hop(own, *parts):
        tail = jnp.where(side == 1, own, jnp.concatenate(parts, axis=2))
        turn = me // 4 % 2

        def pairs(first):
            groups = [[c, (c + 4) % n_ctx] for c in range(n_ctx) if c // 4 % 2 == first]
            return lax.all_to_all(
                jnp.stack([tail, tail]), "ctx", 0, 0, axis_index_groups=groups
            )[0]

        got = pairs(0)
        if n_ctx > 8:
            got = jnp.where(turn == 1, got, pairs(1))
        return got

    last = shard - FAR_ROWS
    blocks = doc_index.reshape(-1, rows)
    tails = [kv_own[:, last:]] + [part[:, last:] for part in kv_other]
    stats, tails = lax.optimization_barrier((stats, tails))
    kv_far = lax.cond(
        jnp.any(blocks[:-2, -1] == blocks[2:, 0]),
        far_hop,
        lambda own, *parts: jnp.zeros_like(own),
        *tails,
    )

    def finished(wave, groups, ids, stats):
        heads = 2 * len(groups)
        width = heads * HD
        return call(
            functools.partial(remote_kernel, groups, shard, pad, wave),
            [((block, width), BF16)] * 4,
            [
                vmem((2, TILE, width), BF16),
                vmem((pad, width), BF16),
                vmem((width, pad), BF16),
                vmem((2 * TILE, width), BF16),
                vmem((2, width, TILE), F32),
                vmem((2, 8, TILE), F32),
                vmem((2, 2 * heads, TILE), F32),
                sems((6,)),
            ],
            5e6 if wave == 0 and groups == (1,) else 1,
            [IN_SMEM, IN_SMEM, IN_VMEM] + [IN_HBM] * 4 + [IN_VMEM] * (2 + len(groups)),
            [ids, docs, docs_row, q_own, q_other, summed, stats, same, kv_far]
            + [crossed[group] for group in groups],
        )

    def exchanged(pieces):
        return [
            pieces[0],
            lax.ppermute(pieces[1], "head", core),
            lax.ppermute(pieces[2], "ctx", swap),
            lax.ppermute(pieces[3], ("ctx", "head"), both),
        ]

    def project(pieces, places, begun, kind, part, parts):
        columns = w_out.shape[1] // parts
        width = pieces[0].shape[1]
        chunk = 512 if begun is None else 1024
        ring = max(2, min(8, RING_VALUES // (width * len(pieces) * chunk)))
        more = [] if begun is None else [begun]
        (out,) = call(
            functools.partial(project_kernel, places, half, ring, part, chunk, begun is not None),
            [((block, columns), kind)],
            [vmem((ring, len(pieces), width, chunk), BF16), sems((ring, len(pieces)))],
            1,
            [IN_SMEM] + [IN_VMEM] * len(pieces) + [IN_HBM] * 2 + [IN_VMEM] * len(more),
            [ids, *pieces, w_out, w_other, *more],
            PROJECT_BYTES,
        )
        return out

    parts = 2
    early = exchanged(finished(0, (0,), ids, stats))
    late = exchanged(finished(0, (1,), ids_late, stats))
    begun = project(
        early[:2] + late[:2] + early[2:],
        ((0, 0), (1, 0), (0, quarter), (1, quarter), (2, 0), (3, 0)),
        None, F32, 0, 1,
    )
    leaving = [
        project(late[2:], ((2, quarter), (3, quarter)), begun, BF16, part, parts)
        for part in range(parts)
    ]
    arrived = [lax.ppermute(part, "head", far_y) for part in leaving]
    stats, leaving = lax.optimization_barrier((stats, leaving))
    pieces = exchanged(finished(1, (0, 1), ids_late, stats))
    staying = project(pieces, tuple((turn, 0) for turn in range(4)), None, F32, 0, 1)
    (out,) = call(
        add_kernel,
        [((block, w_out.shape[1]), BF16)],
        [],
        1,
        [IN_VMEM] * (1 + parts),
        [staying, *arrived],
    )
    return out


def solution(mesh):
    in_specs = (P("ctx", "head"), P(None, "ctx", "head"), P("head", None), P())
    out_specs = P(("ctx", "head"), None)
    return jax.shard_map(
        per_device, mesh=mesh, in_specs=in_specs, out_specs=out_specs, check_vma=False
    )
```
